128 devices in a mesh: region: 8 (over y_hi, x), scan: 16 (over y_lo, z, core).
Axes of the slice: x: 4, y: 4 (y_hi: 2, y_lo: 2; y = y_hi * 2 + y_lo), z: 4, core: 2. Of those that a mesh axis runs over, the one named last changes fastest.
Arguments:
- object_real: float32 [2, 4096, 8192], P(None, 'region', 'scan'), may hold values from 0.25 to 1.75
- object_imag: float32 [2, 4096, 8192], P(None, 'region', 'scan'), may hold values from -1.8 to 1.8
- probe_modes: float32 [2, 2, 128, 128], replicated, may hold values from -6 to 6
- amplitudes: float32 [2048, 128, 128], P(('region', 'scan')), may hold values from 0.5 to 4
- offsets: int32 [2048, 2], P(('region', 'scan')), may hold values from 0 to 384
- owners: int32 [2048, 1], P(('region', 'scan')), may hold values from 0 to 15; in each aligned block of 16 rows (0 to 15, 16 to 31, ...) at most 2 rows name the same one
Outputs:
- object_grad: float32 [2, 2, 4096, 8192], P(None, None, 'region', 'scan')
- probe_grad: float32 [2, 2, 128, 128], replicated
The draws below stay inside these ranges and needn't reach their ends.
Inputs may be any that keep to these rules, and one draw needn't show every extreme that they name: `offsets`: a position's whole patch lies inside the tile that its owner index names. `owners`: each row names a scan index within the region of the device that holds the position; among the 16 rows of one device no index appears more than 2 times, and in every draw some device names some index exactly 2 times.
All inputs are finite; a program needn't handle non-finite values.
Results may differ from the reference program's by a relative error of at most 0.0029.
The reference program's roundings to bfloat16 on the way count: a program that leaves them out, or rounds other values in their place, can miss the bound.
Values may be sent and summed in bfloat16 or wider, within the bound.
No kernel may reach another device: no remote copies, remote signals or barrier semaphores. Data moves between devices by JAX's collectives and lax.ppermute only.
A program may use at most 128 MiB of HBM per device.

```python
import math
import jax
import jax.numpy as jnp
import numpy as np
from jax import lax

PATCH = 128
MODES = 2
SLICES = 2
TILE = 512
CAP = 2
POS_DEV = 16
POSITIONS = 2048
NROWS = 4096
NCOLS = 8192
N_SCAN = 16


def plant(entries, stream_key, least, top_value):
    longest = entries.shape.index(max(entries.shape))
    spots = []
    for shift in (0, 1):
        where = [jax.random.randint(jax.random.fold_in(stream_key, axis), (), 0, length) for axis, length in enumerate(entries.shape)]
        where[longest] = (where[longest] + shift) % entries.shape[longest]
        spots.append(tuple(where))
    return entries.at[spots[0]].set(least).at[spots[1]].set(top_value)


def level_of(rng, dims, cuts, least, top_value):
    gain = 1.0
    for axis_at, blocks in cuts:
        draws = jax.random.uniform(jax.random.fold_in(jax.random.fold_in(rng, 6), axis_at), (blocks,), jnp.float32, least / len(cuts), top_value / len(cuts))
        gain = gain * jnp.repeat(jnp.exp(draws), dims[axis_at] // blocks).reshape((-1,) + (1,) * (len(dims) - 1 - axis_at))
    return gain


def deal_out(stream_key, own, number, rows, number_of, top, reach, skew):
    sequence = jax.random.permutation(stream_key, number_of)
    crowded, common = load_shares(number_of, rows * top, reach, skew, True), load_shares(number_of, rows * top, reach, skew, False)
    places = jnp.arange(number_of)

    def named(sizes, offset_by):
        used = int((sizes > 0).sum())
        fixed = max(1, used // 4)
        shifted = fixed + (places - fixed + offset_by * (used - fixed)) % max(1, number_of - fixed)
        return jnp.zeros((number_of,), jnp.int32).at[sequence[jnp.where(places < fixed, places, shifted)]].set(jnp.asarray(sizes, jnp.int32))

    sizes = jnp.where(number % 4 == 0, named(crowded, number // 4), named(common, number - number // 4 - 1))
    mixed = jax.random.permutation(jax.random.fold_in(own, 3), number_of)
    donor, sink = mixed[0:number_of // 2 * 2:2], mixed[1:number_of // 2 * 2:2]
    slack = jnp.minimum(sizes[donor] - 1, reach - sizes[sink]) // 2
    slack = jnp.where((donor == sequence[0]) | (sink == sequence[0]) | (sizes[sink] == 0), 0, jnp.maximum(slack, 0))
    shifted = jax.random.randint(jax.random.fold_in(own, 4), (number_of // 2,), 0, 1 << 20) % (slack + 1)
    sizes = sizes.at[donor].add(-shifted).at[sink].add(shifted)
    labels = jnp.searchsorted(jnp.cumsum(sizes), jnp.arange(rows * top), side="right").astype(jnp.int32)
    listing = labels.reshape(top, rows).T
    listing = listing[jax.random.permutation(jax.random.fold_in(own, 1), rows)]
    offset_by = jax.random.randint(jax.random.fold_in(own, 2), (rows, 1), 0, top)
    return jnp.take_along_axis(listing, (jnp.arange(top)[None, :] + offset_by) % top, axis=1)


def load_shares(count, total, bound, slope, full):
    portions = [(1 << 20) // math.isqrt(grade ** slope) + 1 for grade in range(1, count + 1)]
    largest = bound if full else min(bound, max(-(-total // count), total * portions[0] // sum(portions)))
    least = 1 if total - largest >= count - 1 else 0
    given, surplus = [largest] + [least] * (count - 1), total - largest - least * (count - 1)
    while surplus > 0:
        movable = [i for i in range(1, count) if given[i] < largest] or [i for i in range(1, count) if given[i] < bound]
        whole, left = sum([portions[i] for i in movable]), surplus
        for i in movable:
            more = min(bound - given[i], max(1, left * portions[i] // whole), surplus)
            given[i] = given[i] + more
            surplus = surplus - more
    return np.array(given)


def bell_draw(stream_key, extent, spread, limit, cuts=(), kind=jnp.bfloat16):
    result = spread * jax.random.normal(stream_key, extent, jnp.float32)
    if cuts:
        result = result * level_of(stream_key, extent, cuts, -0.22, 0.18)
    return jnp.clip(result, -limit, limit).astype(kind)


def setup_inputs(seed: int = 0) -> dict:
    arg_keys = jax.random.split(jax.random.key(seed), 7)
    object_real = jnp.clip(1.0 + 0.15 * jax.random.normal(arg_keys[0], (SLICES, NROWS, NCOLS), jnp.float32), 0.25, 1.75)
    object_imag = bell_draw(arg_keys[1], (SLICES, NROWS, NCOLS), 0.3, 1.8, ((1, 8), (2, 16)), jnp.float32)
    probe_modes = bell_draw(arg_keys[2], (MODES, 2, PATCH, PATCH), 1.0, 6.0, (), jnp.float32)
    amplitudes = jnp.clip(0.5 + 3.5 * jax.random.uniform(arg_keys[3], (POSITIONS, PATCH, PATCH), jnp.float32) ** level_of(arg_keys[3], (POSITIONS, PATCH, PATCH), ((0, 128),), -0.2, 0.2), 0.5, 4.0)
    offsets = plant(jax.random.randint(arg_keys[4], (POSITIONS, 2), 0, TILE - PATCH + 1), jax.random.fold_in(arg_keys[4], 1), 0, TILE - PATCH).astype(jnp.int32)
    owners_keys = jax.random.split(jax.random.fold_in(arg_keys[5], 1), POSITIONS // POS_DEV)
    owners_turns = jax.random.permutation(jax.random.fold_in(arg_keys[5], 3), POSITIONS // POS_DEV)
    owners = jax.vmap(lambda own, number: deal_out(jax.random.fold_in(arg_keys[5], 2), own, number, POS_DEV, N_SCAN, 1, CAP, 2))(owners_keys, owners_turns).reshape((POSITIONS, 1))
    return dict(object_real=object_real, object_imag=object_imag, probe_modes=probe_modes, amplitudes=amplitudes, offsets=offsets, owners=owners)


fresnel_depth = 20.0

def make_kernel(patch_size):
    index = jnp.arange(patch_size, dtype=jnp.int32)
    frequency = ((index + patch_size // 2) % patch_size - patch_size // 2).astype(jnp.float32) / patch_size
    phase = -jnp.pi * fresnel_depth * (frequency[:, None] ** 2 + frequency[None, :] ** 2)
    return lax.complex(jnp.cos(phase), jnp.sin(phase))

def forward_fft(field):
    return jnp.fft.fft2(field, axes=(-2, -1), norm='ortho')

def inverse_fft(field):
    return jnp.fft.ifft2(field, axes=(-2, -1), norm='ortho')

def position_grads(patch, probe_field, measured, kernel):
    incoming = []
    wave = probe_field
    for layer in range(SLICES):
        incoming.append(wave)
        wave = wave * patch[layer]
        if layer + 1 < SLICES:
            wave = inverse_fft(kernel * forward_fft(wave))
    far_field = forward_fft(wave)
    intensity = lax.optimization_barrier(jnp.sum(far_field.real ** 2 + far_field.imag ** 2, axis=0))
    factor = 1.0 - measured / jnp.sqrt(intensity + 1.0)
    back_wave = inverse_fft(far_field * factor)
    grads = [None] * SLICES
    for layer in reversed(range(SLICES)):
        grads[layer] = lax.optimization_barrier(jnp.sum(jnp.conj(incoming[layer]) * back_wave, axis=0))
        back_wave = jnp.conj(patch[layer]) * back_wave
        if layer > 0:
            back_wave = inverse_fft(jnp.conj(kernel) * forward_fft(back_wave))
    return (jnp.stack(grads, axis=0), back_wave)

def to_bf16(values):
    return lax.optimization_barrier(values.astype(jnp.bfloat16)).astype(jnp.float32)

def reference(object_real, object_imag, probe_modes, amplitudes, offsets, owners):
    objs = lax.complex(to_bf16(object_real), to_bf16(object_imag))
    probe_field = lax.complex(probe_modes[:, 0], probe_modes[:, 1])
    kernel = make_kernel(PATCH)
    position_index = jnp.arange(POSITIONS, dtype=jnp.int32)
    region_index = position_index // (POS_DEV * N_SCAN)
    rows_at = (region_index * TILE + offsets[:, 0]).astype(jnp.int32)
    cols_at = (owners[:, 0] * TILE + offsets[:, 1]).astype(jnp.int32)

    def add_position(carry, item):
        grad_real, grad_imag, probe_sum = carry
        row_at, col_at, measured = item
        anchor = jnp.int32(0)
        corner = (anchor, row_at, col_at)
        patch = lax.dynamic_slice(objs, corner, (SLICES, PATCH, PATCH))
        grads, back_wave = position_grads(patch, probe_field, measured, kernel)
        current = lax.dynamic_slice(grad_real, corner, (SLICES, PATCH, PATCH))
        grad_real = lax.dynamic_update_slice(grad_real, current + to_bf16(grads.real), corner)
        current = lax.dynamic_slice(grad_imag, corner, (SLICES, PATCH, PATCH))
        grad_imag = lax.dynamic_update_slice(grad_imag, current + to_bf16(grads.imag), corner)
        return ((grad_real, grad_imag, probe_sum + back_wave), None)
    start_carry = (jnp.zeros((SLICES, NROWS, NCOLS), jnp.float32), jnp.zeros((SLICES, NROWS, NCOLS), jnp.float32), jnp.zeros((MODES, PATCH, PATCH), probe_field.dtype))
    final, unused = lax.scan(add_position, start_carry, (rows_at, cols_at, amplitudes))
    grad_real, grad_imag, probe_sum = final
    object_grad = jnp.stack([grad_real, grad_imag], axis=1).astype(jnp.float32)
    probe_grad = (jnp.stack([probe_sum.real, probe_sum.imag], axis=1) / POS_DEV).astype(jnp.float32)
    return (object_grad, probe_grad)
```

```python
import functools

import jax
import jax.numpy as jnp
import numpy as np
from jax import lax
from jax.experimental import pallas as pl
from jax.experimental.pallas import tpu as pltpu
from jax.sharding import PartitionSpec as P

BF16 = jnp.bfloat16
F32 = jnp.float32
I32 = jnp.int32

CAP = 2
FRESNEL_DEPTH = 20.0
N = 128
TILE = 512
UNROLL = 4
WIN_ROWS = N + 8
AMP_MID = 2.25
AMP_STEP = 1.75 / 32767.0
VMEM_LIMIT = 56 * 2**20


def operator_tables():
    index = np.arange(N)
    transform = np.exp(-2j * np.pi * (np.outer(index, index) % N) / N) / np.sqrt(N)
    frequency = ((index + N // 2) % N - N // 2) / N
    phase = np.exp(-1j * np.pi * FRESNEL_DEPTH * frequency**2)
    move = np.conj(transform) @ (phase[:, None] * transform)
    tables = []
    for matrix in (move, transform):
        right = np.block([[matrix.real, matrix.imag], [-matrix.imag, matrix.real]])
        for form in (right, right.T):
            form = form.astype(np.float32)
            high = form.astype(BF16)
            low = (form - high.astype(np.float32)).astype(BF16)
            tables += [high, low]
    return tables


def split(value):
    high = value.astype(BF16)
    return high, (value - high.astype(F32)).astype(BF16)


def dot(a, b):
    return jnp.dot(a, b, preferred_element_type=F32)


def right_mul(value, table):
    high, low = split(value)
    return dot(high, table[0]) + dot(low, table[0]) + dot(high, table[1])


def left_mul(value, table):
    high, low = split(value)
    return dot(table[0], high) + dot(table[0], low) + dot(table[1], high)


def blocks(value):
    return [[value[:N, :N], value[:N, N:]], [value[N:, :N], value[N:, N:]]]


def join(parts):
    return jnp.concatenate([jnp.concatenate(row, axis=1) for row in parts], axis=0)


def swap(value):
    (a, b), (c, d) = blocks(value)
    return join([[a, c], [b, d]])


def list_live(index_ref, meta):
    def visit(slot, count):
        source, which = slot // CAP, slot % CAP
        row = index_ref[source, 2 * which]
        col = index_ref[source, 2 * which + 1]
        live = (row >= 0).astype(I32)

        @pl.when(live == 1)
        def _():
            meta[0, count] = slot
            meta[1, count] = row
            meta[2, count] = col
            meta[3, count] = which
            meta[4, count] = 1

        return count + live

    slots = index_ref.shape[0] * CAP
    count = lax.fori_loop(0, slots, visit, jnp.int32(0))
    for extra in range(UNROLL):
        meta[0, count + extra] = 0
        meta[1, count + extra] = 0
        meta[2, count + extra] = 0
        meta[3, count + extra] = 0
        meta[4, count + extra] = 0
    return (count + UNROLL - 1) // UNROLL


def requests_kernel(me_ref, owners_ref, offsets_ref, out_ref, target_ref, seen):
    groups = out_ref.shape[0]
    out_ref[...] = jnp.full(out_ref.shape, -1, I32)
    lane = lax.broadcasted_iota(I32, (1, N), 1)
    for owner in range(groups):
        seen[owner] = 0
    for position in range(owners_ref.shape[0]):
        owner = owners_ref[position, 0]
        rank = seen[owner]
        seen[owner] = rank + 1
        core = (owner ^ me_ref[0] ^ rank) & 1
        device = (owner & ~1) | core
        which = (owner & 1) ^ core
        line = out_ref[pl.ds(device, 1), :]
        line = jnp.where(lane == 2 * which, offsets_ref[position, 0], line)
        line = jnp.where(lane == 2 * which + 1, offsets_ref[position, 1], line)
        out_ref[pl.ds(device, 1), :] = line
        target_ref[position] = device * CAP + which


def amplitudes_kernel(target_ref, amplitudes_ref, out_ref):
    def place(position, carry):
        code = jnp.round((amplitudes_ref[position] - AMP_MID) * (1.0 / AMP_STEP))
        out_ref[target_ref[position]] = code.astype(I32).astype(jnp.int16)
        return carry

    lax.fori_loop(0, amplitudes_ref.shape[0], place, 0)


def forward_kernel(
    index_ref, own_re, own_im, mate_re, mate_im, probe_ref, rah, ral, lah, lal, rwh, rwl, lwh, lwl,
    wave_out, far_out, patch_out,
    meta, window, wave_buf, far_buf, patch_buf, window_sem, out_sem,
):
    n_groups = list_live(index_ref, meta)

    def window_copies(group, half, start):
        for u in range(UNROLL):
            item = group * UNROLL + u
            row = pl.multiple_of(jnp.minimum(meta[1, item] // 8 * 8, TILE - WIN_ROWS), 8)
            col = pl.multiple_of(jnp.minimum(meta[2, item] // N, 2) * N, N)
            for tile, sources in enumerate(((own_re, own_im), (mate_re, mate_im))):
                @pl.when(meta[3, item] == tile)
                def _(sources=sources):
                    for part, source in enumerate(sources):
                        for side in range(2):
                            place = pl.ds(pl.multiple_of(col + side * N, N), N)
                            copy = pltpu.make_async_copy(
                                source.at[:, pl.ds(row, WIN_ROWS), place],
                                window.at[half, u, part, side],
                                window_sem.at[half, u, part, side],
                            )
                            copy.start() if start else copy.wait()

    def out_copies(group, half):
        first = group * UNROLL
        pairs = ((wave_buf, wave_out), (far_buf, far_out), (patch_buf, patch_out))
        return [
            pltpu.make_async_copy(buf.at[half], out.at[pl.ds(first, UNROLL)], out_sem.at[half, i])
            for i, (buf, out) in enumerate(pairs)
        ]

    @pl.when(n_groups > 0)
    def _():
        window_copies(0, 0, True)

    lane = lax.broadcasted_iota(I32, (N, N), 1)

    def step(group, carry):
        half = lax.rem(group, 2)

        @pl.when(group + 1 < n_groups)
        def _():
            window_copies(group + 1, 1 - half, True)

        window_copies(group, half, False)

        @pl.when(group >= 2)
        def _():
            for copy in out_copies(group - 2, half):
                copy.wait()

        waves = []
        for u in range(UNROLL):
            item = group * UNROLL + u
            row, col = meta[1, item], meta[2, item]
            row_in = row - jnp.minimum(row // 8 * 8, TILE - WIN_ROWS)
            shift = col - jnp.minimum(col // N, 2) * N
            back = lax.rem(N - shift, N)
            for layer in range(2):
                for part in range(2):
                    first = window[half, u, part, 0, layer, pl.ds(row_in, N), :]
                    second = window[half, u, part, 1, layer, pl.ds(row_in, N), :]
                    cut = jnp.where(
                        lane < N - shift, pltpu.roll(first, back, 1), pltpu.roll(second, back, 1)
                    )
                    patch_buf[half, u, 2 * layer + part] = cut.astype(BF16)
            p_re = patch_buf[half, u, 0].astype(F32)
            p_im = patch_buf[half, u, 1].astype(F32)
            rows = []
            for mode in range(2):
                w_re, w_im = probe_ref[mode, 0], probe_ref[mode, 1]
                rows.append([w_re * p_re - w_im * p_im, w_re * p_im + w_im * p_re])
            waves.append(join(rows))
        waves = [right_mul(w, (rah[...], ral[...])) for w in waves]
        waves = [left_mul(swap(w), (lah[...], lal[...])) for w in waves]
        for u in range(UNROLL):
            wave_buf[half, u] = waves[u]
            p_re = patch_buf[half, u, 2].astype(F32)
            p_im = patch_buf[half, u, 3].astype(F32)
            w = blocks(waves[u])
            waves[u] = join(
                [
                    [w[0][m] * p_re - w[1][m] * p_im, w[0][m] * p_im + w[1][m] * p_re]
                    for m in range(2)
                ]
            )
        waves = [right_mul(w, (rwh[...], rwl[...])) for w in waves]
        waves = [left_mul(swap(w), (lwh[...], lwl[...])) for w in waves]
        for u in range(UNROLL):
            far_buf[half, u] = waves[u]
        for copy in out_copies(group, half):
            copy.start()
        return carry

    lax.fori_loop(0, n_groups, step, 0)
    for before in (2, 1):

        @pl.when(n_groups >= before)
        def _(before=before):
            for copy in out_copies(n_groups - before, lax.rem(n_groups - before, 2)):
                copy.wait()


def backward_kernel(
    index_ref, codes_ref, wave_in, far_in, patch_in, probe_ref, rah, ral, lah, lal, rwh, rwl, lwh, lwl,
    own_out, mate_out, probe_out,
    meta, total, wave_buf, far_buf, patch_buf, in_sem, out_sem,
):
    n_groups = list_live(index_ref, meta)

    def in_copies(group, half):
        first = group * UNROLL
        pairs = ((wave_in, wave_buf), (far_in, far_buf), (patch_in, patch_buf))
        return [
            pltpu.make_async_copy(src.at[pl.ds(first, UNROLL)], buf.at[half], in_sem.at[half, i])
            for i, (src, buf) in enumerate(pairs)
        ]

    @pl.when(n_groups > 0)
    def _():
        for copy in in_copies(0, 0):
            copy.start()

    total[...] = jnp.zeros(total.shape, F32)
    probe_out[...] = jnp.zeros(probe_out.shape, F32)
    lane = lax.broadcasted_iota(I32, (N, N), 1)

    def add_patch(item, plane, value):
        row, col, tile = meta[1, item], meta[2, item], meta[3, item]
        first = jnp.minimum(col // N, 2)
        shift = col - first * N
        moved = pltpu.roll(value.astype(BF16).astype(F32), lax.rem(shift, N), 1)
        here = (tile, plane, first, pl.ds(row, N))
        there = (tile, plane, first + 1, pl.ds(row, N))
        total[here] = total[here] + jnp.where(lane >= shift, moved, 0.0)
        total[there] = total[there] + jnp.where(lane < shift, moved, 0.0)

    def step(group, carry):
        half = lax.rem(group, 2)

        @pl.when(group + 1 < n_groups)
        def _():
            for copy in in_copies(group + 1, 1 - half):
                copy.start()

        for copy in in_copies(group, half):
            copy.wait()

        waves = []
        for u in range(UNROLL):
            item = group * UNROLL + u
            far = blocks(far_buf[half, u])
            intensity = sum(far[c][m] * far[c][m] for c in range(2) for m in range(2))
            code = codes_ref[meta[0, item]].astype(I32).astype(F32)
            measured = code * AMP_STEP + AMP_MID
            factor = (1.0 - measured * lax.rsqrt(intensity + 1.0)) * meta[4, item].astype(F32)
            waves.append(join([[far[c][m] * factor for m in range(2)] for c in range(2)]))
        waves = [left_mul(w, (rwh[...], rwl[...])) for w in waves]
        waves = [right_mul(swap(w), (lwh[...], lwl[...])) for w in waves]
        for u in range(UNROLL):
            item = group * UNROLL + u
            back = blocks(waves[u])
            wave = blocks(wave_buf[half, u])
            add_patch(
                item, 2, sum(wave[0][m] * back[m][0] + wave[1][m] * back[m][1] for m in range(2))
            )
            add_patch(
                item, 3, sum(wave[0][m] * back[m][1] - wave[1][m] * back[m][0] for m in range(2))
            )
            p_re = patch_buf[half, u, 2].astype(F32)
            p_im = patch_buf[half, u, 3].astype(F32)
            waves[u] = join(
                [
                    [
                        p_re * back[m][0] + p_im * back[m][1],
                        p_re * back[m][1] - p_im * back[m][0],
                    ]
                    for m in range(2)
                ]
            )
        waves = [right_mul(w, (lah[...], lal[...])) for w in waves]
        waves = [left_mul(swap(w), (rah[...], ral[...])) for w in waves]
        terms = [[0.0, 0.0], [0.0, 0.0]]
        for u in range(UNROLL):
            item = group * UNROLL + u
            back = blocks(waves[u])
            probe = [[probe_ref[m, c] for c in range(2)] for m in range(2)]
            add_patch(
                item, 0, sum(probe[m][0] * back[0][m] + probe[m][1] * back[1][m] for m in range(2))
            )
            add_patch(
                item, 1, sum(probe[m][0] * back[1][m] - probe[m][1] * back[0][m] for m in range(2))
            )
            p_re = patch_buf[half, u, 0].astype(F32)
            p_im = patch_buf[half, u, 1].astype(F32)
            for m in range(2):
                terms[m][0] = terms[m][0] + (p_re * back[0][m] + p_im * back[1][m])
                terms[m][1] = terms[m][1] + (p_re * back[1][m] - p_im * back[0][m])
        for m in range(2):
            for c in range(2):
                probe_out[m, c] += terms[m][c]
        return carry

    lax.fori_loop(0, n_groups, step, 0)
    copies = [
        pltpu.make_async_copy(
            total.at[tile, pl.ds(2 * layer, 2), side],
            out.at[layer, :, :, pl.ds(side * N, N)],
            out_sem.at[tile, layer, side],
        )
        for tile, out in enumerate((own_out, mate_out))
        for layer in range(2)
        for side in range(TILE // N)
    ]
    for copy in copies:
        copy.start()
    for copy in copies:
        copy.wait()


def spec(space):
    return pl.BlockSpec(memory_space=space)


def reduce_probe(part):
    axes = ("region", "scan")
    devices = lax.axis_size("region") * lax.axis_size("scan")
    chips = devices // 2
    mates = [(i, i ^ 1) for i in range(devices)]
    same_core = [list(range(core, devices, 2)) for core in range(2)]
    core = lax.axis_index("scan") & 1
    halves = part.reshape(2, chips, -1)
    kept = lax.dynamic_index_in_dim(halves, core, 0, False)
    given = lax.dynamic_index_in_dim(halves, 1 - core, 0, False)
    mine = kept + lax.ppermute(given, axes, mates)
    pieces = lax.all_to_all(mine, axes, 0, 0, axis_index_groups=same_core, tiled=True)
    piece = jnp.sum(pieces, axis=0, keepdims=True)
    half = lax.all_to_all(
        jnp.broadcast_to(piece, pieces.shape), axes, 0, 0, axis_index_groups=same_core, tiled=True
    )
    other = lax.ppermute(half, axes, mates)
    whole = jnp.where(core == 0, jnp.stack([half, other]), jnp.stack([other, half]))
    return whole.reshape(part.shape)


def body(object_real, object_imag, probe_modes, amplitudes, offsets, owners):
    groups = lax.axis_size("scan")
    pos_dev = offsets.shape[0]
    slots = groups * CAP
    vmem, smem, anywhere = spec(pltpu.VMEM), spec(pltpu.SMEM), spec(pl.ANY)
    params = pltpu.CompilerParams(vmem_limit_bytes=VMEM_LIMIT)
    mates = [(i, i ^ 1) for i in range(groups)]
    tables = [jnp.asarray(t) for t in operator_tables()]
    me = lax.axis_index("scan").astype(I32).reshape(1)

    requests, target = pl.pallas_call(
        requests_kernel,
        out_shape=(
            jax.ShapeDtypeStruct((groups, N), I32),
            jax.ShapeDtypeStruct((pos_dev,), I32),
        ),
        in_specs=[smem, smem, smem],
        out_specs=(vmem, smem),
        scratch_shapes=[pltpu.SMEM((groups,), I32)],
        name="requests",
    )(me, owners, offsets)
    arrived = lax.all_to_all(requests, "scan", 0, 0, tiled=True)
    mate_real = lax.ppermute(object_real, "scan", mates)
    mate_imag = lax.ppermute(object_imag, "scan", mates)
    codes = pl.pallas_call(
        amplitudes_kernel,
        out_shape=jax.ShapeDtypeStruct((slots, N, N), jnp.int16),
        in_specs=[smem, vmem],
        out_specs=vmem,
        compiler_params=params,
        name="amplitudes",
    )(target, amplitudes)
    codes = lax.all_to_all(
        codes.reshape(groups, CAP, N, N), "scan", 0, 0, tiled=True
    ).reshape(slots, N, N)

    two = 2 * N
    flops = slots * 4 * 3 * 2 * two**3
    waves, fars, patches = pl.pallas_call(
        forward_kernel,
        out_shape=(
            jax.ShapeDtypeStruct((slots, two, two), F32),
            jax.ShapeDtypeStruct((slots, two, two), F32),
            jax.ShapeDtypeStruct((slots, 4, N, N), BF16),
        ),
        in_specs=[smem] + [anywhere] * 4 + [vmem] * 9,
        out_specs=(anywhere,) * 3,
        scratch_shapes=[
            pltpu.SMEM((5, slots + UNROLL), I32),
            pltpu.VMEM((2, UNROLL, 2, 2, 2, WIN_ROWS, N), F32),
            pltpu.VMEM((2, UNROLL, two, two), F32),
            pltpu.VMEM((2, UNROLL, two, two), F32),
            pltpu.VMEM((2, UNROLL, 4, N, N), BF16),
            pltpu.SemaphoreType.DMA((2, UNROLL, 2, 2)),
            pltpu.SemaphoreType.DMA((2, 3)),
        ],
        compiler_params=params,
        cost_estimate=pl.CostEstimate(flops=flops, bytes_accessed=40 * 2**20, transcendentals=0),
        name="forward",
    )(arrived, object_real, object_imag, mate_real, mate_imag, probe_modes, *tables)
    grad_shape = jax.ShapeDtypeStruct((2, 2, TILE, TILE), F32)
    own_grad, mate_grad, probe_part = pl.pallas_call(
        backward_kernel,
        out_shape=(grad_shape, grad_shape, jax.ShapeDtypeStruct((2, 2, N, N), F32)),
        in_specs=[smem, vmem] + [anywhere] * 3 + [vmem] * 9,
        out_specs=(anywhere, anywhere, vmem),
        scratch_shapes=[
            pltpu.SMEM((5, slots + UNROLL), I32),
            pltpu.VMEM((2, 4, TILE // N, TILE, N), F32),
            pltpu.VMEM((2, UNROLL, two, two), F32),
            pltpu.VMEM((2, UNROLL, two, two), F32),
            pltpu.VMEM((2, UNROLL, 4, N, N), BF16),
            pltpu.SemaphoreType.DMA((2, 3)),
            pltpu.SemaphoreType.DMA((2, 2, TILE // N)),
        ],
        compiler_params=params,
        cost_estimate=pl.CostEstimate(flops=flops, bytes_accessed=40 * 2**20, transcendentals=0),
        name="backward",
    )(arrived, codes, waves, fars, patches, probe_modes, *tables)
    object_grad = own_grad + lax.ppermute(mate_grad, "scan", mates)
    return object_grad, reduce_probe(probe_part) / pos_dev


def solution(mesh):
    return jax.shard_map(
        body,
        mesh=mesh,
        in_specs=(
            P(None, "region", "scan"),
            P(None, "region", "scan"),
            P(),
            P(("region", "scan"), None, None),
            P(("region", "scan"), None),
            P(("region", "scan"), None),
        ),
        out_specs=(P(None, None, "region", "scan"), P()),
        check_vma=False,
    )
```

```python
import functools

import jax
import jax.numpy as jnp
import numpy as np
from jax import lax
from jax.experimental import pallas as pl
from jax.experimental.pallas import tpu as pltpu
from jax.sharding import PartitionSpec as P

BF16 = jnp.bfloat16
F32 = jnp.float32
I32 = jnp.int32

CAP = 2
FRESNEL_DEPTH = 20.0
N = 128
TILE = 512
UNROLL = 4
WIN_ROWS = N + 8
TAIL = 16
AMP_MID = 2.25
AMP_STEP = 1.75 / 32767.0
VMEM_LIMIT = 56 * 2**20


def operator_tables():
    index = np.arange(N)
    transform = np.exp(-2j * np.pi * (np.outer(index, index) % N) / N) / np.sqrt(N)
    frequency = ((index + N // 2) % N - N // 2) / N
    phase = np.exp(-1j * np.pi * FRESNEL_DEPTH * frequency**2)
    move = np.conj(transform) @ (phase[:, None] * transform)
    tables = []
    for matrix in (move, transform):
        right = np.block([[matrix.real, matrix.imag], [-matrix.imag, matrix.real]])
        for form in (right, right.T):
            form = form.astype(np.float32)
            high = form.astype(BF16)
            low = (form - high.astype(np.float32)).astype(BF16)
            tables += [high, low]
    return tables


def split(value):
    high = value.astype(BF16)
    return high, (value - high.astype(F32)).astype(BF16)


def dot(a, b):
    return jnp.dot(a, b, preferred_element_type=F32)


def right_mul(value, table):
    high, low = split(value)
    return dot(high, table[0]) + dot(low, table[0]) + dot(high, table[1])


def left_mul(value, table):
    high, low = split(value)
    return dot(table[0], high) + dot(table[0], low) + dot(table[1], high)


def blocks(value):
    return [[value[:N, :N], value[:N, N:]], [value[N:, :N], value[N:, N:]]]


def join(parts):
    return jnp.concatenate([jnp.concatenate(row, axis=1) for row in parts], axis=0)


def list_live(corner_ref, meta):
    slots = corner_ref.shape[0] // 2

    def visit(which):
        def look(source, count):
            slot = source * CAP + which
            row = corner_ref[2 * slot]
            live = (row >= 0).astype(I32)

            @pl.when(live == 1)
            def _():
                meta[0, count] = slot
                meta[1, count] = row
                meta[2, count] = corner_ref[2 * slot + 1]
                meta[3, count] = which
                meta[4, count] = 1

            return count + live

        return look

    n_mate = lax.fori_loop(0, slots // CAP, visit(1), jnp.int32(0))
    count = lax.fori_loop(0, slots // CAP, visit(0), n_mate)
    for extra in range(UNROLL):
        for field in range(5):
            meta[field, count + extra] = 0
    return n_mate, count


def prepare_kernel(me_ref, owners_ref, offsets_ref, amplitudes_ref, out_ref, seen):
    for owner in range(out_ref.shape[0] // CAP):
        seen[owner] = 0
    out_ref[:, N:, :] = jnp.full((out_ref.shape[0], TAIL, N), -1, jnp.int16)
    lane = lax.broadcasted_iota(I32, (TAIL, N), 1)

    def place(position, carry):
        owner = owners_ref[position]
        rank = seen[owner]
        seen[owner] = rank + 1
        core = (owner ^ me_ref[0] ^ rank) & 1
        slot = ((owner & ~1) | core) * CAP + ((owner & 1) ^ core)
        code = jnp.round((amplitudes_ref[position] - AMP_MID) * (1.0 / AMP_STEP))
        out_ref[slot, :N, :] = code.astype(I32).astype(jnp.int16)
        line = jnp.where(lane == 0, offsets_ref[0, position], -1)
        line = jnp.where(lane == 1, offsets_ref[1, position], line)
        out_ref[slot, N:, :] = line.astype(jnp.int16)
        return carry

    lax.fori_loop(0, amplitudes_ref.shape[0], place, 0)


def positions_kernel(
    corner_ref, codes_ref, own_re, own_im, mate_re, mate_im, probe_ref,
    rah, ral, lah, lal, rwh, rwl, lwh, lwl,
    own_out, mate_out, probe_out,
    meta, window, patch, high, low, field, inner, back, total, window_sem, out_sem,
):
    n_mate, count = list_live(corner_ref, meta)
    n_groups = (count + UNROLL - 1) // UNROLL
    mate_last = jnp.maximum((n_mate + UNROLL - 1) // UNROLL - 1, 0)

    def window_copies(group, half, start):
        for u in range(UNROLL):
            item = group * UNROLL + u
            row = pl.multiple_of(jnp.minimum(meta[1, item] // 8 * 8, TILE - WIN_ROWS), 8)
            col = pl.multiple_of(jnp.minimum(meta[2, item] // N, 2) * N, N)
            for tile, sources in enumerate(((own_re, own_im), (mate_re, mate_im))):

                @pl.when(meta[3, item] == tile)
                def _(sources=sources, u=u, row=row, col=col):
                    for part, source in enumerate(sources):
                        for side in range(2):
                            place = pl.ds(pl.multiple_of(col + side * N, N), N)
                            copy = pltpu.make_async_copy(
                                source.at[:, pl.ds(row, WIN_ROWS), place],
                                window.at[half, u, part, side],
                                window_sem.at[half, u, part, side],
                            )
                            copy.start() if start else copy.wait()

    def total_copies(tile):
        out = (own_out, mate_out)[tile]
        return [
            pltpu.make_async_copy(
                total.at[tile, pl.ds(2 * layer, 2), side],
                out.at[layer, :, :, pl.ds(side * N, N)],
                out_sem.at[tile, layer, side],
            )
            for layer in range(2)
            for side in range(TILE // N)
        ]

    @pl.when(n_groups > 0)
    def _():
        window_copies(0, 0, True)

    total[...] = jnp.zeros(total.shape, F32)
    probe_out[...] = jnp.zeros(probe_out.shape, F32)
    lane = lax.broadcasted_iota(I32, (N, N), 1)
    lo, hi = pl.ds(0, N), pl.ds(N, N)
    halves = (lo, hi)

    def step(group, carry):
        buffer = lax.rem(group, 2)

        @pl.when(group + 1 < n_groups)
        def _():
            window_copies(group + 1, 1 - buffer, True)

        window_copies(group, buffer, False)
        items = [group * UNROLL + u for u in range(UNROLL)]
        where = []
        for item in items:
            row, col = meta[1, item], meta[2, item]
            first = jnp.minimum(col // N, 2)
            shift = col - first * N
            row_in = row - jnp.minimum(row // 8 * 8, TILE - WIN_ROWS)
            where.append((meta[3, item], row, row_in, first, shift))

        def put(u, r, c, value):
            big, small = split(value)
            high[u, halves[r], halves[c]] = big
            low[u, halves[r], halves[c]] = small

        def cut(u, layer, part):
            def piece():
                _, _, row_in, _, shift = where[u]
                move = lax.rem(N - shift, N)
                near = window[buffer, u, part, 0, layer, pl.ds(row_in, N), :]
                far = window[buffer, u, part, 1, layer, pl.ds(row_in, N), :]
                both = jnp.where(lane < N - shift, pltpu.roll(near, move, 1), pltpu.roll(far, move, 1))
                patch[u, 2 * layer + part] = both.astype(BF16).astype(F32)

            return piece

        def swap_blocks(u, source):
            def piece(r, c):
                return lambda: put(u, r, c, source[u, halves[c], halves[r]])

            return [piece(r, c) for r in range(2) for c in range(2)]

        def times_patch(u, layer, load, sign):
            def piece(m, c):
                def work():
                    p_re, p_im = patch[u, 2 * layer], patch[u, 2 * layer + 1]
                    if c == 0:
                        put(u, m, 0, load(m, 0) * p_re - sign * (load(m, 1) * p_im))
                    else:
                        put(u, m, 1, load(m, 1) * p_re + sign * (load(m, 0) * p_im))

                return work

            return [piece(m, c) for m in range(2) for c in range(2)]

        def residual(u):
            def factor():
                power = sum(field[u, halves[c], halves[m]] ** 2 for c in range(2) for m in range(2))
                code = codes_ref[meta[0, items[u]], :N, :].astype(I32).astype(F32)
                measured = code * AMP_STEP + AMP_MID
                live = meta[4, items[u]].astype(F32)
                inner_factor[u] = (1.0 - measured * lax.rsqrt(power + 1.0)) * live

            def piece(c, m):
                return lambda: put(u, c, m, field[u, halves[c], halves[m]] * inner_factor[u])

            return [factor] + [piece(c, m) for c in range(2) for m in range(2)]

        inner_factor = {}

        def add_patch(u, plane, value):
            tile, row, _, first, shift = where[u]
            moved = pltpu.roll(value.astype(BF16).astype(F32), lax.rem(shift, N), 1)
            here = (tile, plane, first, pl.ds(row, N))
            there = (tile, plane, first + 1, pl.ds(row, N))
            total[here] = total[here] + jnp.where(lane >= shift, moved, 0.0)
            total[there] = total[there] + jnp.where(lane < shift, moved, 0.0)

        def exit_gradient(u):
            def wave(c, m):
                return inner[u, halves[c], halves[m]]

            def wake(c, m):
                return back[u, halves[m], halves[c]]

            return [
                lambda: add_patch(
                    u, 2, sum(wave(0, m) * wake(0, m) + wave(1, m) * wake(1, m) for m in range(2))
                ),
                lambda: add_patch(
                    u, 3, sum(wave(0, m) * wake(1, m) - wave(1, m) * wake(0, m) for m in range(2))
                ),
            ]

        def entry_gradient(u):
            def wake(c, m):
                return field[u, halves[c], halves[m]]

            def probe_term(m):
                def work():
                    p_re, p_im = patch[u, 0], patch[u, 1]
                    probe_out[m, 0] += p_re * wake(0, m) + p_im * wake(1, m)
                    probe_out[m, 1] += p_re * wake(1, m) - p_im * wake(0, m)

                return work

            return [
                probe_term(0),
                probe_term(1),
                lambda: add_patch(
                    u,
                    0,
                    sum(
                        probe_ref[m, 0] * wake(0, m) + probe_ref[m, 1] * wake(1, m) for m in range(2)
                    ),
                ),
                lambda: add_patch(
                    u,
                    1,
                    sum(
                        probe_ref[m, 0] * wake(1, m) - probe_ref[m, 1] * wake(0, m) for m in range(2)
                    ),
                ),
            ]

        def from_probe(u):
            return lambda m, c: probe_ref[m, c]

        def from_inner(u):
            return lambda m, c: inner[u, halves[c], halves[m]]

        def from_back(u):
            return lambda m, c: back[u, halves[m], halves[c]]

        stages = (
            ("right", rah, ral, field, lambda u: [cut(u, 0, 0), cut(u, 0, 1)] + times_patch(u, 0, from_probe(u), 1), lambda u: []),
            ("left", lah, lal, inner, lambda u: swap_blocks(u, field), lambda u: [cut(u, 1, 0), cut(u, 1, 1)]),
            ("right", rwh, rwl, field, lambda u: times_patch(u, 1, from_inner(u), 1), lambda u: []),
            ("left", lwh, lwl, field, lambda u: swap_blocks(u, field), lambda u: []),
            ("left", rwh, rwl, field, residual, lambda u: []),
            ("right", lwh, lwl, back, lambda u: swap_blocks(u, field), lambda u: []),
            ("right", lah, lal, field, lambda u: times_patch(u, 1, from_back(u), -1), lambda u: []),
            ("left", rah, ral, field, lambda u: swap_blocks(u, field), exit_gradient),
        )
        jobs = [(s, u) for s in range(len(stages)) for u in range(UNROLL)]
        for piece in stages[0][4](0):
            piece()
        for at, (s, u) in enumerate(jobs):
            side, table_high, table_low, result, _, beside = stages[s]
            pieces = list(beside(u))
            if at + 1 < len(jobs):
                s_next, u_next = jobs[at + 1]
                pieces = list(stages[s_next][4](u_next)) + pieces
            if s == len(stages) - 1 and u > 0:
                pieces += entry_gradient(u - 1)
            cuts = [(len(pieces) * k + 2) // 3 for k in range(4)]
            big, small = high[u], low[u]
            sums = None
            for k, (data, table) in enumerate(((big, table_high), (small, table_high), (big, table_low))):
                product = dot(data, table[...]) if side == "right" else dot(table[...], data)
                sums = product if sums is None else sums + product
                for piece in pieces[cuts[k] : cuts[k + 1]]:
                    piece()
            result[u] = sums
        for piece in entry_gradient(UNROLL - 1):
            piece()

        @pl.when(group == mate_last)
        def _():
            for copy in total_copies(1):
                copy.start()

        return carry

    lax.fori_loop(0, n_groups, step, 0)

    @pl.when(n_groups == 0)
    def _():
        for copy in total_copies(1):
            copy.start()

    for copy in total_copies(0):
        copy.start()
    for copy in total_copies(0) + total_copies(1):
        copy.wait()


def spec(space):
    return pl.BlockSpec(memory_space=space)


VMEM, SMEM, ANY = spec(pltpu.VMEM), spec(pltpu.SMEM), spec(pl.ANY)
PARAMS = pltpu.CompilerParams(vmem_limit_bytes=VMEM_LIMIT)
TWO = 2 * N


def run_positions(corners, codes, own_re, own_im, mate_re, mate_im, probe, tables):
    slots = codes.shape[0]
    grad_shape = jax.ShapeDtypeStruct((2, 2, TILE, TILE), F32)
    wave = pltpu.VMEM((UNROLL, TWO, TWO), F32)
    half = pltpu.VMEM((UNROLL, TWO, TWO), BF16)
    return pl.pallas_call(
        positions_kernel,
        out_shape=(grad_shape, grad_shape, jax.ShapeDtypeStruct((2, 2, N, N), F32)),
        in_specs=[SMEM, VMEM] + [ANY] * 4 + [VMEM] * 9,
        out_specs=(ANY, ANY, VMEM),
        scratch_shapes=[
            pltpu.SMEM((5, slots + UNROLL), I32),
            pltpu.VMEM((2, UNROLL, 2, 2, 2, WIN_ROWS, N), F32),
            pltpu.VMEM((UNROLL, 4, N, N), F32),
            half,
            half,
            wave,
            wave,
            wave,
            pltpu.VMEM((2, 4, TILE // N, TILE, N), F32),
            pltpu.SemaphoreType.DMA((2, UNROLL, 2, 2)),
            pltpu.SemaphoreType.DMA((2, 2, TILE // N)),
        ],
        compiler_params=PARAMS,
        cost_estimate=pl.CostEstimate(
            flops=slots * 48 * TWO**3, bytes_accessed=24 * 2**20, transcendentals=0
        ),
        name="positions",
    )(corners, codes, own_re, own_im, mate_re, mate_im, probe, *tables)


def tie(*values):
    return lax.optimization_barrier(values)


def finish(own_grad, mate_grad, probe_part):
    axes = ("region", "scan")
    devices = lax.axis_size("region") * lax.axis_size("scan")
    chips = devices // 2
    mates = [(i, i ^ 1) for i in range(devices)]
    same_core = [list(range(core, devices, 2)) for core in range(2)]
    core = lax.axis_index("scan") & 1
    halves = probe_part.reshape(2, chips, -1)
    kept = lax.dynamic_index_in_dim(halves, core, 0, False)
    given = lax.dynamic_index_in_dim(halves, 1 - core, 0, False)
    mine = kept + lax.ppermute(given, axes, mates)
    mine, mate_grad = tie(mine, mate_grad)
    other_grad = lax.ppermute(mate_grad, axes, mates)
    pieces = lax.all_to_all(mine, axes, 0, 0, axis_index_groups=same_core, tiled=True)
    piece = jnp.sum(pieces, axis=0, keepdims=True)
    piece, other_grad = tie(piece, other_grad)
    half = lax.all_to_all(
        jnp.broadcast_to(piece, pieces.shape), axes, 0, 0, axis_index_groups=same_core, tiled=True
    )
    object_grad = own_grad + other_grad
    half, object_grad = tie(half, object_grad)
    other = lax.ppermute(half, axes, mates)
    whole = jnp.where(core == 0, jnp.stack([half, other]), jnp.stack([other, half]))
    return object_grad, whole.reshape(probe_part.shape)


def body(object_real, object_imag, probe_modes, amplitudes, offsets, owners):
    groups = lax.axis_size("scan")
    pos_dev = offsets.shape[0]
    slots = groups * CAP
    mates = [(i, i ^ 1) for i in range(groups)]
    tables = [jnp.asarray(t) for t in operator_tables()]
    me = lax.axis_index("scan").astype(I32).reshape(1)

    requests = pl.pallas_call(
        prepare_kernel,
        out_shape=jax.ShapeDtypeStruct((slots, N + TAIL, N), jnp.int16),
        in_specs=[SMEM, SMEM, SMEM, VMEM],
        out_specs=VMEM,
        scratch_shapes=[pltpu.SMEM((groups,), I32)],
        compiler_params=PARAMS,
        name="prepare",
    )(me, owners.reshape(pos_dev), offsets.T, amplitudes)
    arrived = lax.all_to_all(
        requests.reshape(groups, CAP, N + TAIL, N), "scan", 0, 0, tiled=True
    ).reshape(slots, N + TAIL, N)
    mate_real = lax.ppermute(object_real, "scan", mates)
    mate_imag = lax.ppermute(object_imag, "scan", mates)
    corners = arrived[:, N, :2].astype(I32).reshape(2 * slots)
    own_grad, mate_grad, probe_part = run_positions(
        corners, arrived, object_real, object_imag, mate_real, mate_imag, probe_modes, tables
    )
    object_grad, probe_grad = finish(own_grad, mate_grad, probe_part)
    return object_grad, probe_grad / pos_dev


def solution(mesh):
    return jax.shard_map(
        body,
        mesh=mesh,
        in_specs=(
            P(None, "region", "scan"),
            P(None, "region", "scan"),
            P(),
            P(("region", "scan"), None, None),
            P(("region", "scan"), None),
            P(("region", "scan"), None),
        ),
        out_specs=(P(None, None, "region", "scan"), P()),
        check_vma=False,
    )
```

```python
import functools

import jax
import jax.numpy as jnp
import numpy as np
from jax import lax
from jax.experimental import pallas as pl
from jax.experimental.pallas import tpu as pltpu
from jax.sharding import PartitionSpec as P

BF16 = jnp.bfloat16
F32 = jnp.float32
I32 = jnp.int32

CAP = 2
FRESNEL_DEPTH = 20.0
N = 128
TILE = 512
UNROLL = 4
WIN_ROWS = N + 8
TAIL = 16
AMP_MID = 2.25
AMP_STEP = 1.75 / 32767.0
VMEM_LIMIT = 56 * 2**20


def operator_tables():
    index = np.arange(N)
    transform = np.exp(-2j * np.pi * (np.outer(index, index) % N) / N) / np.sqrt(N)
    frequency = ((index + N // 2) % N - N // 2) / N
    phase = np.exp(-1j * np.pi * FRESNEL_DEPTH * frequency**2)
    move = np.conj(transform) @ (phase[:, None] * transform)
    tables = []
    for matrix in (move, transform):
        right = np.block([[matrix.real, matrix.imag], [-matrix.imag, matrix.real]])
        for form in (right, right.T):
            form = form.astype(np.float32)
            high = form.astype(BF16)
            low = (form - high.astype(np.float32)).astype(BF16)
            tables += [high, low]
    return tables


def split(value):
    high = value.astype(BF16)
    return high, (value - high.astype(F32)).astype(BF16)


def dot(a, b):
    return jnp.dot(a, b, preferred_element_type=F32)


def right_mul(value, table):
    high, low = split(value)
    return dot(high, table[0]) + dot(low, table[0]) + dot(high, table[1])


def left_mul(value, table):
    high, low = split(value)
    return dot(table[0], high) + dot(table[0], low) + dot(table[1], high)


def blocks(value):
    return [[value[:N, :N], value[:N, N:]], [value[N:, :N], value[N:, N:]]]


def join(parts):
    return jnp.concatenate([jnp.concatenate(row, axis=1) for row in parts], axis=0)


def list_live(corner_ref, meta):
    slots = corner_ref.shape[0]

    def visit(which):
        def look(source, count):
            slot = source * CAP + which
            row = corner_ref[slot, 0]
            live = (row >= 0).astype(I32)

            @pl.when(live == 1)
            def _():
                meta[0, count] = slot
                meta[1, count] = row
                meta[2, count] = corner_ref[slot, 1]
                meta[3, count] = which
                meta[4, count] = 1

            return count + live

        return look

    n_mate = lax.fori_loop(0, slots // CAP, visit(1), jnp.int32(0))
    count = lax.fori_loop(0, slots // CAP, visit(0), n_mate)
    for extra in range(UNROLL):
        for field in range(5):
            meta[field, count + extra] = 0
    return n_mate, count


def prepare_kernel(me_ref, owners_ref, offsets_ref, amplitudes_ref, out_ref, seen):
    for owner in range(out_ref.shape[0] // CAP):
        seen[owner] = 0
    out_ref[:, N:, :] = jnp.full((out_ref.shape[0], TAIL, N), -1, jnp.int16)
    lane = lax.broadcasted_iota(I32, (TAIL, N), 1)

    def place(position, carry):
        owner = owners_ref[position]
        rank = seen[owner]
        seen[owner] = rank + 1
        core = (owner ^ me_ref[0] ^ rank) & 1
        slot = ((owner & ~1) | core) * CAP + ((owner & 1) ^ core)
        code = jnp.round((amplitudes_ref[position] - AMP_MID) * (1.0 / AMP_STEP))
        out_ref[slot, :N, :] = code.astype(I32).astype(jnp.int16)
        line = jnp.where(lane == 0, offsets_ref[0, position], -1)
        line = jnp.where(lane == 1, offsets_ref[1, position], line)
        out_ref[slot, N:, :] = line.astype(jnp.int16)
        return carry

    lax.fori_loop(0, amplitudes_ref.shape[0], place, 0)


def positions_kernel(
    corner_ref, codes_ref, own_re, own_im, mate_re, mate_im, probe_in, tables_ref,
    own_out, mate_out, probe_out,
    meta, window, code, patch, high, low, field, inner, back, total, tables, probe_ref, probe_total,
    window_sem, code_sem, out_sem, table_sem, probe_sem,
):
    table_copy = pltpu.make_async_copy(tables_ref, tables, table_sem)
    table_copy.start()
    probe_copy = pltpu.make_async_copy(probe_in, probe_ref, probe_sem.at[0])
    probe_copy.start()
    n_mate, count = list_live(corner_ref, meta)
    n_groups = (count + UNROLL - 1) // UNROLL
    mate_last = jnp.maximum((n_mate + UNROLL - 1) // UNROLL - 1, 0)

    def window_copies(group, half, start):
        for u in range(UNROLL):
            item = group * UNROLL + u
            row = pl.multiple_of(jnp.minimum(meta[1, item] // 8 * 8, TILE - WIN_ROWS), 8)
            col = pl.multiple_of(jnp.minimum(meta[2, item] // N, 2) * N, N)
            for tile, sources in enumerate(((own_re, own_im), (mate_re, mate_im))):

                @pl.when(meta[3, item] == tile)
                def _(sources=sources, u=u, row=row, col=col):
                    for part, source in enumerate(sources):
                        for side in range(2):
                            place = pl.ds(pl.multiple_of(col + side * N, N), N)
                            copy = pltpu.make_async_copy(
                                source.at[:, pl.ds(row, WIN_ROWS), place],
                                window.at[half, u, part, side],
                                window_sem.at[half, u, part, side],
                            )
                            copy.start() if start else copy.wait()

            copy = pltpu.make_async_copy(
                codes_ref.at[meta[0, item], pl.ds(0, N)], code.at[half, u], code_sem.at[half, u]
            )
            copy.start() if start else copy.wait()

    def total_copies(tile):
        out = (own_out, mate_out)[tile]
        return [
            pltpu.make_async_copy(
                total.at[tile, pl.ds(2 * layer, 2), side],
                out.at[layer, :, :, pl.ds(side * N, N)],
                out_sem.at[tile, layer, side],
            )
            for layer in range(2)
            for side in range(TILE // N)
        ]

    @pl.when(n_groups > 0)
    def _():
        window_copies(0, 0, True)

    total[...] = jnp.zeros(total.shape, F32)
    probe_total[...] = jnp.zeros(probe_total.shape, F32)
    lane = lax.broadcasted_iota(I32, (N, N), 1)
    halves = (pl.ds(0, N), pl.ds(N, N))
    table_copy.wait()
    probe_copy.wait()

    def step(group, carry):
        buffer = lax.rem(group, 2)

        @pl.when(group + 1 < n_groups)
        def _():
            window_copies(group + 1, 1 - buffer, True)

        window_copies(group, buffer, False)
        items = [group * UNROLL + u for u in range(UNROLL)]
        where = []
        for item in items:
            row, col = meta[1, item], meta[2, item]
            first = jnp.minimum(col // N, 2)
            shift = col - first * N
            row_in = row - jnp.minimum(row // 8 * 8, TILE - WIN_ROWS)
            where.append((meta[3, item], row, row_in, first, shift))

        def put(u, r, c, value):
            big, small = split(value)
            high[u, halves[r], halves[c]] = big
            low[u, halves[r], halves[c]] = small

        def cut(u, layer, part):
            def piece():
                _, _, row_in, _, shift = where[u]
                move = lax.rem(N - shift, N)
                near = window[buffer, u, part, 0, layer, pl.ds(row_in, N), :]
                far = window[buffer, u, part, 1, layer, pl.ds(row_in, N), :]
                both = jnp.where(lane < N - shift, pltpu.roll(near, move, 1), pltpu.roll(far, move, 1))
                patch[u, 2 * layer + part] = both.astype(BF16).astype(F32)

            return piece

        def swap_blocks(u, source):
            def piece(r, c):
                return lambda: put(u, r, c, source[u, halves[c], halves[r]])

            return [piece(r, c) for r in range(2) for c in range(2)]

        def times_patch(u, layer, load, sign):
            def piece(m, c):
                def work():
                    p_re, p_im = patch[u, 2 * layer], patch[u, 2 * layer + 1]
                    if c == 0:
                        put(u, m, 0, load(m, 0) * p_re - sign * (load(m, 1) * p_im))
                    else:
                        put(u, m, 1, load(m, 1) * p_re + sign * (load(m, 0) * p_im))

                return work

            return [piece(m, c) for m in range(2) for c in range(2)]

        def residual(u):
            def factor():
                power = sum(field[u, halves[c], halves[m]] ** 2 for c in range(2) for m in range(2))
                measured = code[buffer, u].astype(I32).astype(F32) * AMP_STEP + AMP_MID
                live = meta[4, items[u]].astype(F32)
                inner_factor[u] = (1.0 - measured * lax.rsqrt(power + 1.0)) * live

            def piece(c, m):
                return lambda: put(u, c, m, field[u, halves[c], halves[m]] * inner_factor[u])

            return [factor] + [piece(c, m) for c in range(2) for m in range(2)]

        inner_factor = {}

        def add_patch(u, plane, value):
            tile, row, _, first, shift = where[u]
            moved = pltpu.roll(value.astype(BF16).astype(F32), lax.rem(shift, N), 1)
            here = (tile, plane, first, pl.ds(row, N))
            there = (tile, plane, first + 1, pl.ds(row, N))
            total[here] = total[here] + jnp.where(lane >= shift, moved, 0.0)
            total[there] = total[there] + jnp.where(lane < shift, moved, 0.0)

        def exit_gradient(u):
            def wave(c, m):
                return inner[u, halves[c], halves[m]]

            def wake(c, m):
                return back[u, halves[m], halves[c]]

            return [
                lambda: add_patch(
                    u, 2, sum(wave(0, m) * wake(0, m) + wave(1, m) * wake(1, m) for m in range(2))
                ),
                lambda: add_patch(
                    u, 3, sum(wave(0, m) * wake(1, m) - wave(1, m) * wake(0, m) for m in range(2))
                ),
            ]

        def entry_gradient(u):
            def wake(c, m):
                return field[u, halves[c], halves[m]]

            def probe_term(m):
                def work():
                    p_re, p_im = patch[u, 0], patch[u, 1]
                    probe_total[m, 0] += p_re * wake(0, m) + p_im * wake(1, m)
                    probe_total[m, 1] += p_re * wake(1, m) - p_im * wake(0, m)

                return work

            return [
                probe_term(0),
                probe_term(1),
                lambda: add_patch(
                    u,
                    0,
                    sum(
                        probe_ref[m, 0] * wake(0, m) + probe_ref[m, 1] * wake(1, m) for m in range(2)
                    ),
                ),
                lambda: add_patch(
                    u,
                    1,
                    sum(
                        probe_ref[m, 0] * wake(1, m) - probe_ref[m, 1] * wake(0, m) for m in range(2)
                    ),
                ),
            ]

        def from_probe(u):
            return lambda m, c: probe_ref[m, c]

        def from_inner(u):
            return lambda m, c: inner[u, halves[c], halves[m]]

        def from_back(u):
            return lambda m, c: back[u, halves[m], halves[c]]

        stages = (
            ("right", 0, field, lambda u: [cut(u, 0, 0), cut(u, 0, 1)] + times_patch(u, 0, from_probe(u), 1), lambda u: []),
            ("left", 1, inner, lambda u: swap_blocks(u, field), lambda u: [cut(u, 1, 0), cut(u, 1, 1)]),
            ("right", 2, field, lambda u: times_patch(u, 1, from_inner(u), 1), lambda u: []),
            ("left", 3, field, lambda u: swap_blocks(u, field), lambda u: []),
            ("left", 2, field, residual, lambda u: []),
            ("right", 3, back, lambda u: swap_blocks(u, field), lambda u: []),
            ("right", 1, field, lambda u: times_patch(u, 1, from_back(u), -1), lambda u: []),
            ("left", 0, field, lambda u: swap_blocks(u, field), exit_gradient),
        )
        jobs = [(s, u) for s in range(len(stages)) for u in range(UNROLL)]
        for piece in stages[0][3](0):
            piece()
        for at, (s, u) in enumerate(jobs):
            side, form, result, _, beside = stages[s]
            pieces = list(beside(u))
            if at + 1 < len(jobs):
                s_next, u_next = jobs[at + 1]
                pieces = list(stages[s_next][3](u_next)) + pieces
            if s == len(stages) - 1 and u > 0:
                pieces += entry_gradient(u - 1)
            cuts = [(len(pieces) * k + 2) // 3 for k in range(4)]
            big, small = high[u], low[u]
            sums = None
            for k, (data, part) in enumerate(((big, 0), (small, 0), (big, 1))):
                table = tables[2 * form + part]
                product = dot(data, table) if side == "right" else dot(table, data)
                sums = product if sums is None else sums + product
                for piece in pieces[cuts[k] : cuts[k + 1]]:
                    piece()
            result[u] = sums
        for piece in entry_gradient(UNROLL - 1):
            piece()

        @pl.when(group == mate_last)
        def _():
            for copy in total_copies(1):
                copy.start()

        return carry

    lax.fori_loop(0, n_groups, step, 0)

    @pl.when(n_groups == 0)
    def _():
        for copy in total_copies(1):
            copy.start()

    probe_back = pltpu.make_async_copy(probe_total, probe_out, probe_sem.at[1])
    for copy in total_copies(0) + [probe_back]:
        copy.start()
    for copy in total_copies(0) + total_copies(1) + [probe_back]:
        copy.wait()


def spec(space):
    return pl.BlockSpec(memory_space=space)


VMEM, SMEM, HBM, ANY = spec(pltpu.VMEM), spec(pltpu.SMEM), spec(pltpu.HBM), spec(pl.ANY)
PARAMS = pltpu.CompilerParams(vmem_limit_bytes=VMEM_LIMIT)
TWO = 2 * N


def run_positions(corners, codes, own_re, own_im, mate_re, mate_im, probe, tables):
    slots = codes.shape[0]
    grad_shape = jax.ShapeDtypeStruct((2, 2, TILE, TILE), F32)
    wave = pltpu.VMEM((UNROLL, TWO, TWO), F32)
    half = pltpu.VMEM((UNROLL, TWO, TWO), BF16)
    return pl.pallas_call(
        positions_kernel,
        out_shape=(grad_shape, grad_shape, jax.ShapeDtypeStruct((2, 2, N, N), F32)),
        in_specs=[SMEM] + [ANY] * 3 + [HBM] * 2 + [ANY] * 2,
        out_specs=(ANY, ANY, ANY),
        scratch_shapes=[
            pltpu.SMEM((5, slots + UNROLL), I32),
            pltpu.VMEM((2, UNROLL, 2, 2, 2, WIN_ROWS, N), F32),
            pltpu.VMEM((2, UNROLL, N, N), jnp.int16),
            pltpu.VMEM((UNROLL, 4, N, N), F32),
            half,
            half,
            wave,
            wave,
            wave,
            pltpu.VMEM((2, 4, TILE // N, TILE, N), F32),
            pltpu.VMEM((8, TWO, TWO), BF16),
            pltpu.VMEM((2, 2, N, N), F32),
            pltpu.VMEM((2, 2, N, N), F32),
            pltpu.SemaphoreType.DMA((2, UNROLL, 2, 2)),
            pltpu.SemaphoreType.DMA((2, UNROLL)),
            pltpu.SemaphoreType.DMA((2, 2, TILE // N)),
            pltpu.SemaphoreType.DMA,
            pltpu.SemaphoreType.DMA((2,)),
        ],
        compiler_params=PARAMS,
        cost_estimate=pl.CostEstimate(
            flops=slots * 48 * TWO**3, bytes_accessed=24 * 2**20, transcendentals=0
        ),
        name="positions",
    )(corners, codes, own_re, own_im, mate_re, mate_im, probe, tables)


def tie(*values):
    return lax.optimization_barrier(values)


def finish(own_grad, mate_grad, probe_part, pos_dev):
    axes = ("region", "scan")
    devices = lax.axis_size("region") * lax.axis_size("scan")
    mates = [(i, i ^ 1) for i in range(devices)]
    other_grad = lax.ppermute(mate_grad, axes, mates)
    parts = probe_part.reshape(devices, -1, N)
    pieces = lax.all_to_all(parts, axes, 0, 0, tiled=True)
    piece = jnp.sum(pieces, axis=0, keepdims=True) / pos_dev
    piece, other_grad = tie(piece, other_grad)
    whole = lax.all_to_all(jnp.broadcast_to(piece, parts.shape), axes, 0, 0, tiled=True)
    object_grad = own_grad + other_grad
    whole, object_grad = tie(whole, object_grad)
    return object_grad, whole.reshape(probe_part.shape)


def body(object_real, object_imag, probe_modes, amplitudes, offsets, owners):
    groups = lax.axis_size("scan")
    pos_dev = offsets.shape[0]
    slots = groups * CAP
    mates = [(i, i ^ 1) for i in range(groups)]
    tables = jnp.asarray(np.stack(operator_tables()))
    me = lax.axis_index("scan").astype(I32).reshape(1)

    requests = pl.pallas_call(
        prepare_kernel,
        out_shape=jax.ShapeDtypeStruct((slots, N + TAIL, N), jnp.int16),
        in_specs=[SMEM, SMEM, SMEM, VMEM],
        out_specs=VMEM,
        scratch_shapes=[pltpu.SMEM((groups,), I32)],
        compiler_params=PARAMS,
        name="prepare",
    )(me, owners.reshape(pos_dev), offsets.T, amplitudes)
    arrived = lax.all_to_all(
        requests.reshape(groups, CAP, N + TAIL, N), "scan", 0, 0, tiled=True
    ).reshape(slots, N + TAIL, N)
    mate_real = lax.ppermute(object_real, "scan", mates)
    mate_imag = lax.ppermute(object_imag, "scan", mates)
    corners = arrived[:, N, :2].astype(I32)
    own_grad, mate_grad, probe_part = run_positions(
        corners, arrived, object_real, object_imag, mate_real, mate_imag, probe_modes, tables
    )
    return finish(own_grad, mate_grad, probe_part, pos_dev)


def solution(mesh):
    return jax.shard_map(
        body,
        mesh=mesh,
        in_specs=(
            P(None, "region", "scan"),
            P(None, "region", "scan"),
            P(),
            P(("region", "scan"), None, None),
            P(("region", "scan"), None),
            P(("region", "scan"), None),
        ),
        out_specs=(P(None, None, "region", "scan"), P()),
        check_vma=False,
    )
```

```python
import functools

import jax
import jax.numpy as jnp
import numpy as np
from jax import lax
from jax.experimental import pallas as pl
from jax.experimental.pallas import tpu as pltpu
from jax.sharding import PartitionSpec as P

BF16 = jnp.bfloat16
F32 = jnp.float32
I32 = jnp.int32

CAP = 2
FRESNEL_DEPTH = 20.0
N = 128
TILE = 512
UNROLL = 4
WIN_ROWS = N + 8
TAIL = 16
AMP_MID = 2.25
AMP_STEP = 1.75 / 32767.0
VMEM_LIMIT = 56 * 2**20


def operator_tables():
    index = np.arange(N)
    transform = np.exp(-2j * np.pi * (np.outer(index, index) % N) / N) / np.sqrt(N)
    frequency = ((index + N // 2) % N - N // 2) / N
    phase = np.exp(-1j * np.pi * FRESNEL_DEPTH * frequency**2)
    move = np.conj(transform) @ (phase[:, None] * transform)
    tables = []
    for matrix in (move, transform):
        right = np.block([[matrix.real, matrix.imag], [-matrix.imag, matrix.real]])
        for form in (right, right.T):
            form = form.astype(np.float32)
            high = form.astype(BF16)
            low = (form - high.astype(np.float32)).astype(BF16)
            tables += [high, low]
    return tables


def split(value):
    high = value.astype(BF16)
    return high, (value - high.astype(F32)).astype(BF16)


def dot(a, b):
    return jnp.dot(a, b, preferred_element_type=F32)


def right_mul(value, table):
    high, low = split(value)
    return dot(high, table[0]) + dot(low, table[0]) + dot(high, table[1])


def left_mul(value, table):
    high, low = split(value)
    return dot(table[0], high) + dot(table[0], low) + dot(table[1], high)


def blocks(value):
    return [[value[:N, :N], value[:N, N:]], [value[N:, :N], value[N:, N:]]]


def join(parts):
    return jnp.concatenate([jnp.concatenate(row, axis=1) for row in parts], axis=0)


def list_live(corner_ref, meta):
    slots = corner_ref.shape[0]

    def visit(which):
        def look(source, count):
            slot = source * CAP + which
            row = corner_ref[slot, 0]
            live = (row >= 0).astype(I32)

            @pl.when(live == 1)
            def _():
                meta[0, count] = slot
                meta[1, count] = row
                meta[2, count] = corner_ref[slot, 1]
                meta[3, count] = which
                meta[4, count] = 1

            return count + live

        return look

    n_mate = lax.fori_loop(0, slots // CAP, visit(1), jnp.int32(0))
    count = lax.fori_loop(0, slots // CAP, visit(0), n_mate)
    for extra in range(UNROLL):
        for field in range(5):
            meta[field, count + extra] = 0
    return n_mate, count


def prepare_kernel(me_ref, owners_ref, offsets_ref, amplitudes_ref, out_ref, seen):
    for owner in range(out_ref.shape[0] // CAP):
        seen[owner] = 0
    out_ref[:, N:, :] = jnp.full((out_ref.shape[0], TAIL, N), -1, jnp.int16)
    lane = lax.broadcasted_iota(I32, (TAIL, N), 1)

    def place(position, carry):
        owner = owners_ref[position]
        rank = seen[owner]
        seen[owner] = rank + 1
        core = (owner ^ me_ref[0] ^ rank) & 1
        slot = ((owner & ~1) | core) * CAP + ((owner & 1) ^ core)
        code = jnp.round((amplitudes_ref[position] - AMP_MID) * (1.0 / AMP_STEP))
        out_ref[slot, :N, :] = code.astype(I32).astype(jnp.int16)
        line = jnp.where(lane == 0, offsets_ref[0, position], -1)
        line = jnp.where(lane == 1, offsets_ref[1, position], line)
        out_ref[slot, N:, :] = line.astype(jnp.int16)
        return carry

    lax.fori_loop(0, amplitudes_ref.shape[0], place, 0)


def round_kernel(own_re, own_im, mate_re, mate_im, out_ref):
    for tile, sources in enumerate(((own_re, own_im), (mate_re, mate_im))):

        @pl.when(pl.program_id(0) == tile)
        def _(sources=sources):
            for part, source in enumerate(sources):
                out_ref[0, 0, part] = source[...].astype(BF16).astype(F32)


def positions_kernel(
    corner_ref, codes_ref, tiles_ref, probe_in, tables_ref,
    grad_out, probe_out,
    meta, window, code, patch, high, low, field, inner, back, grad, tables, probe_ref, probe_total,
    window_sem, code_sem, out_sem, table_sem, probe_sem,
):
    table_copy = pltpu.make_async_copy(tables_ref, tables, table_sem)
    table_copy.start()
    probe_copy = pltpu.make_async_copy(probe_in, probe_ref, probe_sem.at[0])
    probe_copy.start()
    _, count = list_live(corner_ref, meta)
    n_groups = (count + UNROLL - 1) // UNROLL

    def window_copies(group, half, start):
        for u in range(UNROLL):
            item = group * UNROLL + u
            row = pl.multiple_of(jnp.minimum(meta[1, item] // 8 * 8, TILE - WIN_ROWS), 8)
            col = jnp.minimum(meta[2, item] // N, 2)
            copy = pltpu.make_async_copy(
                tiles_ref.at[meta[3, item], pl.ds(col, 2), :, :, pl.ds(row, WIN_ROWS)],
                window.at[half, u],
                window_sem.at[half, u],
            )
            copy.start() if start else copy.wait()
            copy = pltpu.make_async_copy(
                codes_ref.at[meta[0, item], pl.ds(0, N)], code.at[half, u], code_sem.at[half, u]
            )
            copy.start() if start else copy.wait()

    def grad_copy(group, half):
        return pltpu.make_async_copy(
            grad.at[half], grad_out.at[pl.ds(group * UNROLL, UNROLL)], out_sem.at[half]
        )

    @pl.when(n_groups > 0)
    def _():
        window_copies(0, 0, True)

    probe_total[...] = jnp.zeros(probe_total.shape, F32)
    lane = lax.broadcasted_iota(I32, (N, N), 1)
    halves = (pl.ds(0, N), pl.ds(N, N))
    table_copy.wait()
    probe_copy.wait()

    def step(group, carry):
        buffer = lax.rem(group, 2)

        @pl.when(group + 1 < n_groups)
        def _():
            window_copies(group + 1, 1 - buffer, True)

        window_copies(group, buffer, False)

        @pl.when(group >= 2)
        def _():
            grad_copy(group - 2, buffer).wait()

        items = [group * UNROLL + u for u in range(UNROLL)]
        where = []
        for item in items:
            row, col = meta[1, item], meta[2, item]
            shift = col - jnp.minimum(col // N, 2) * N
            row_in = row - jnp.minimum(row // 8 * 8, TILE - WIN_ROWS)
            where.append((row_in, shift))

        def put(u, r, c, value):
            big, small = split(value)
            high[u, halves[r], halves[c]] = big
            low[u, halves[r], halves[c]] = small

        def cut(u, layer, part):
            def piece():
                row_in, shift = where[u]
                move = lax.rem(N - shift, N)
                near = window[buffer, u, 0, part, layer, pl.ds(row_in, N), :]
                far = window[buffer, u, 1, part, layer, pl.ds(row_in, N), :]
                both = jnp.where(lane < N - shift, pltpu.roll(near, move, 1), pltpu.roll(far, move, 1))
                patch[u, 2 * layer + part] = both

            return piece

        def swap_blocks(u, source):
            def piece(r, c):
                return lambda: put(u, r, c, source[u, halves[c], halves[r]])

            return [piece(r, c) for r in range(2) for c in range(2)]

        def times_patch(u, layer, load, sign):
            def piece(m, c):
                def work():
                    p_re, p_im = patch[u, 2 * layer], patch[u, 2 * layer + 1]
                    if c == 0:
                        put(u, m, 0, load(m, 0) * p_re - sign * (load(m, 1) * p_im))
                    else:
                        put(u, m, 1, load(m, 1) * p_re + sign * (load(m, 0) * p_im))

                return work

            return [piece(m, c) for m in range(2) for c in range(2)]

        def residual(u):
            def factor():
                power = sum(field[u, halves[c], halves[m]] ** 2 for c in range(2) for m in range(2))
                measured = code[buffer, u].astype(I32).astype(F32) * AMP_STEP + AMP_MID
                live = meta[4, items[u]].astype(F32)
                inner_factor[u] = (1.0 - measured * lax.rsqrt(power + 1.0)) * live

            def piece(c, m):
                return lambda: put(u, c, m, field[u, halves[c], halves[m]] * inner_factor[u])

            return [factor] + [piece(c, m) for c in range(2) for m in range(2)]

        inner_factor = {}

        def add_patch(u, plane, value):
            grad[buffer, u, plane] = value.astype(BF16)

        def exit_gradient(u):
            def wave(c, m):
                return inner[u, halves[c], halves[m]]

            def wake(c, m):
                return back[u, halves[m], halves[c]]

            return [
                lambda: add_patch(
                    u, 2, sum(wave(0, m) * wake(0, m) + wave(1, m) * wake(1, m) for m in range(2))
                ),
                lambda: add_patch(
                    u, 3, sum(wave(0, m) * wake(1, m) - wave(1, m) * wake(0, m) for m in range(2))
                ),
            ]

        def entry_gradient(u):
            def wake(c, m):
                return field[u, halves[c], halves[m]]

            def probe_term(m):
                def work():
                    p_re, p_im = patch[u, 0], patch[u, 1]
                    probe_total[m, 0] += p_re * wake(0, m) + p_im * wake(1, m)
                    probe_total[m, 1] += p_re * wake(1, m) - p_im * wake(0, m)

                return work

            return [
                probe_term(0),
                probe_term(1),
                lambda: add_patch(
                    u,
                    0,
                    sum(
                        probe_ref[m, 0] * wake(0, m) + probe_ref[m, 1] * wake(1, m) for m in range(2)
                    ),
                ),
                lambda: add_patch(
                    u,
                    1,
                    sum(
                        probe_ref[m, 0] * wake(1, m) - probe_ref[m, 1] * wake(0, m) for m in range(2)
                    ),
                ),
            ]

        def from_probe(u):
            return lambda m, c: probe_ref[m, c]

        def from_inner(u):
            return lambda m, c: inner[u, halves[c], halves[m]]

        def from_back(u):
            return lambda m, c: back[u, halves[m], halves[c]]

        stages = (
            ("right", 0, field, lambda u: [cut(u, 0, 0), cut(u, 0, 1)] + times_patch(u, 0, from_probe(u), 1), lambda u: []),
            ("left", 1, inner, lambda u: swap_blocks(u, field), lambda u: [cut(u, 1, 0), cut(u, 1, 1)]),
            ("right", 2, field, lambda u: times_patch(u, 1, from_inner(u), 1), lambda u: []),
            ("left", 3, field, lambda u: swap_blocks(u, field), lambda u: []),
            ("left", 2, field, residual, lambda u: []),
            ("right", 3, back, lambda u: swap_blocks(u, field), lambda u: []),
            ("right", 1, field, lambda u: times_patch(u, 1, from_back(u), -1), lambda u: []),
            ("left", 0, field, lambda u: swap_blocks(u, field), exit_gradient),
        )
        jobs = [(s, u) for s in range(len(stages)) for u in range(UNROLL)]
        for piece in stages[0][3](0):
            piece()
        for at, (s, u) in enumerate(jobs):
            side, form, result, _, beside = stages[s]
            pieces = list(beside(u))
            if at + 1 < len(jobs):
                s_next, u_next = jobs[at + 1]
                pieces = list(stages[s_next][3](u_next)) + pieces
            if s == len(stages) - 1 and u > 0:
                pieces += entry_gradient(u - 1)
            cuts = [(len(pieces) * k + 2) // 3 for k in range(4)]
            big, small = high[u], low[u]
            sums = None
            for k, (data, part) in enumerate(((big, 0), (small, 0), (big, 1))):
                table = tables[2 * form + part]
                product = dot(data, table) if side == "right" else dot(table, data)
                sums = product if sums is None else sums + product
                for piece in pieces[cuts[k] : cuts[k + 1]]:
                    piece()
            result[u] = sums
        for piece in entry_gradient(UNROLL - 1):
            piece()

        grad_copy(group, buffer).start()
        return carry

    lax.fori_loop(0, n_groups, step, 0)
    probe_back = pltpu.make_async_copy(probe_total, probe_out, probe_sem.at[1])
    probe_back.start()
    for before in (2, 1):

        @pl.when(n_groups >= before)
        def _(before=before):
            grad_copy(n_groups - before, lax.rem(n_groups - before, 2)).wait()

    probe_back.wait()


def scatter_kernel(corner_ref, grad_in, own_out, mate_out, meta, grad, total, in_sem, out_sem):
    n_mate, count = list_live(corner_ref, meta)
    n_groups = (count + UNROLL - 1) // UNROLL
    mate_last = jnp.maximum((n_mate + UNROLL - 1) // UNROLL - 1, 0)

    def grad_copy(group, half):
        return pltpu.make_async_copy(
            grad_in.at[pl.ds(group * UNROLL, UNROLL)], grad.at[half], in_sem.at[half]
        )

    def total_copies(tile):
        out = (own_out, mate_out)[tile]
        return [
            pltpu.make_async_copy(
                total.at[tile, pl.ds(2 * layer, 2), side],
                out.at[layer, :, :, pl.ds(side * N, N)],
                out_sem.at[tile, layer, side],
            )
            for layer in range(2)
            for side in range(TILE // N)
        ]

    @pl.when(n_groups > 0)
    def _():
        grad_copy(0, 0).start()

    total[...] = jnp.zeros(total.shape, F32)
    lane = lax.broadcasted_iota(I32, (N, N), 1)

    def step(group, carry):
        half = lax.rem(group, 2)

        @pl.when(group + 1 < n_groups)
        def _():
            grad_copy(group + 1, 1 - half).start()

        grad_copy(group, half).wait()
        for u in range(UNROLL):
            item = group * UNROLL + u
            row, col, tile = meta[1, item], meta[2, item], meta[3, item]
            first = jnp.minimum(col // N, 2)
            shift = col - first * N
            for plane in range(4):
                moved = pltpu.roll(grad[half, u, plane].astype(F32), lax.rem(shift, N), 1)
                here = (tile, plane, first, pl.ds(row, N))
                there = (tile, plane, first + 1, pl.ds(row, N))
                total[here] = total[here] + jnp.where(lane >= shift, moved, 0.0)
                total[there] = total[there] + jnp.where(lane < shift, moved, 0.0)

        @pl.when(group == mate_last)
        def _():
            for copy in total_copies(1):
                copy.start()

        return carry

    lax.fori_loop(0, n_groups, step, 0)

    @pl.when(n_groups == 0)
    def _():
        for copy in total_copies(1):
            copy.start()

    for copy in total_copies(0):
        copy.start()
    for copy in total_copies(0) + total_copies(1):
        copy.wait()


def spec(space):
    return pl.BlockSpec(memory_space=space)


VMEM, SMEM, HBM, ANY = spec(pltpu.VMEM), spec(pltpu.SMEM), spec(pltpu.HBM), spec(pl.ANY)
PARAMS = pltpu.CompilerParams(vmem_limit_bytes=VMEM_LIMIT)
TWO = 2 * N


def run_round(own_re, own_im, mate_re, mate_im):
    strips = TILE // N

    def index_of(tile):
        idle = strips - 1 if tile == 0 else 0
        return lambda t, strip: (0, 0, jnp.where(t == tile, strip, idle))

    block = (2, TILE, N)
    return pl.pallas_call(
        round_kernel,
        grid=(2, strips),
        out_shape=jax.ShapeDtypeStruct((2, strips, 2, 2, TILE, N), F32),
        in_specs=[pl.BlockSpec(block, index_of(tile)) for tile in (0, 0, 1, 1)],
        out_specs=pl.BlockSpec((1, 1, 2, 2, TILE, N), lambda t, strip: (t, strip, 0, 0, 0, 0)),
        compiler_params=PARAMS,
        cost_estimate=pl.CostEstimate(flops=0, bytes_accessed=16 * 2**20, transcendentals=0),
        name="round",
    )(own_re, own_im, mate_re, mate_im)


def run_positions(corners, codes, tiles, probe, tables):
    slots = codes.shape[0]
    wave = pltpu.VMEM((UNROLL, TWO, TWO), F32)
    half = pltpu.VMEM((UNROLL, TWO, TWO), BF16)
    return pl.pallas_call(
        positions_kernel,
        out_shape=(
            jax.ShapeDtypeStruct((slots, 4, N, N), BF16),
            jax.ShapeDtypeStruct((2, 2, N, N), F32),
        ),
        in_specs=[SMEM] + [ANY] * 4,
        out_specs=(ANY, ANY),
        scratch_shapes=[
            pltpu.SMEM((5, slots + UNROLL), I32),
            pltpu.VMEM((2, UNROLL, 2, 2, 2, WIN_ROWS, N), F32),
            pltpu.VMEM((2, UNROLL, N, N), jnp.int16),
            pltpu.VMEM((UNROLL, 4, N, N), F32),
            half,
            half,
            wave,
            wave,
            wave,
            pltpu.VMEM((2, UNROLL, 4, N, N), BF16),
            pltpu.VMEM((8, TWO, TWO), BF16),
            pltpu.VMEM((2, 2, N, N), F32),
            pltpu.VMEM((2, 2, N, N), F32),
            pltpu.SemaphoreType.DMA((2, UNROLL)),
            pltpu.SemaphoreType.DMA((2, UNROLL)),
            pltpu.SemaphoreType.DMA((2,)),
            pltpu.SemaphoreType.DMA,
            pltpu.SemaphoreType.DMA((2,)),
        ],
        compiler_params=PARAMS,
        cost_estimate=pl.CostEstimate(
            flops=slots * 48 * TWO**3, bytes_accessed=24 * 2**20, transcendentals=0
        ),
        name="positions",
    )(corners, codes, tiles, probe, tables)


def run_scatter(corners, grads):
    slots = grads.shape[0]
    grad_shape = jax.ShapeDtypeStruct((2, 2, TILE, TILE), F32)
    return pl.pallas_call(
        scatter_kernel,
        out_shape=(grad_shape, grad_shape),
        in_specs=[SMEM, ANY],
        out_specs=(ANY, ANY),
        scratch_shapes=[
            pltpu.SMEM((5, slots + UNROLL), I32),
            pltpu.VMEM((2, UNROLL, 4, N, N), BF16),
            pltpu.VMEM((2, 4, TILE // N, TILE, N), F32),
            pltpu.SemaphoreType.DMA((2,)),
            pltpu.SemaphoreType.DMA((2, 2, TILE // N)),
        ],
        compiler_params=PARAMS,
        cost_estimate=pl.CostEstimate(flops=0, bytes_accessed=20 * 2**20, transcendentals=0),
        name="scatter",
    )(corners, grads)


def tie(*values):
    return lax.optimization_barrier(values)


def finish(corners, grads, probe_part, pos_dev):
    axes = ("region", "scan")
    devices = lax.axis_size("region") * lax.axis_size("scan")
    mates = [(i, i ^ 1) for i in range(devices)]
    parts = probe_part.reshape(devices, -1, N)
    own_grad, mate_grad = run_scatter(corners, grads)
    pieces = lax.all_to_all(parts, axes, 0, 0, tiled=True)
    piece = jnp.sum(pieces, axis=0, keepdims=True) / pos_dev
    piece, own_grad, mate_grad = tie(piece, own_grad, mate_grad)
    other_grad = lax.ppermute(mate_grad, axes, mates)
    whole = lax.all_to_all(jnp.broadcast_to(piece, parts.shape), axes, 0, 0, tiled=True)
    object_grad = own_grad + other_grad
    whole, object_grad = tie(whole, object_grad)
    return object_grad, whole.reshape(probe_part.shape)


def body(object_real, object_imag, probe_modes, amplitudes, offsets, owners):
    groups = lax.axis_size("scan")
    pos_dev = offsets.shape[0]
    slots = groups * CAP
    mates = [(i, i ^ 1) for i in range(groups)]
    tables = jnp.asarray(np.stack(operator_tables()))
    me = lax.axis_index("scan").astype(I32).reshape(1)

    requests = pl.pallas_call(
        prepare_kernel,
        out_shape=jax.ShapeDtypeStruct((slots, N + TAIL, N), jnp.int16),
        in_specs=[SMEM, SMEM, SMEM, VMEM],
        out_specs=VMEM,
        scratch_shapes=[pltpu.SMEM((groups,), I32)],
        compiler_params=PARAMS,
        name="prepare",
    )(me, owners.reshape(pos_dev), offsets.T, amplitudes)
    arrived = lax.all_to_all(
        requests.reshape(groups, CAP, N + TAIL, N), "scan", 0, 0, tiled=True
    ).reshape(slots, N + TAIL, N)
    mate_real = lax.ppermute(object_real, "scan", mates)
    mate_imag = lax.ppermute(object_imag, "scan", mates)
    tiles = run_round(object_real, object_imag, mate_real, mate_imag)
    arrived, tiles = tie(arrived, tiles)
    corners = arrived[:, N, :2].astype(I32)
    grads, probe_part = run_positions(
        corners, arrived, tiles, probe_modes, tables
    )
    return finish(corners, grads, probe_part, pos_dev)


def solution(mesh):
    return jax.shard_map(
        body,
        mesh=mesh,
        in_specs=(
            P(None, "region", "scan"),
            P(None, "region", "scan"),
            P(),
            P(("region", "scan"), None, None),
            P(("region", "scan"), None),
            P(("region", "scan"), None),
        ),
        out_specs=(P(None, None, "region", "scan"), P()),
        check_vma=False,
    )
```

```python
import functools

import jax
import jax.numpy as jnp
import numpy as np
from jax import lax
from jax.experimental import pallas as pl
from jax.experimental.pallas import tpu as pltpu
from jax.sharding import PartitionSpec as P

BF16 = jnp.bfloat16
F32 = jnp.float32
I32 = jnp.int32

CAP = 2
FRESNEL_DEPTH = 20.0
N = 128
TILE = 512
UNROLL = 4
WIN_ROWS = N + 8
TAIL = 16
AMP_MID = 2.25
AMP_STEP = 1.75 / 32767.0
VMEM_LIMIT = 56 * 2**20


def operator_tables():
    index = np.arange(N)
    transform = np.exp(-2j * np.pi * (np.outer(index, index) % N) / N) / np.sqrt(N)
    frequency = ((index + N // 2) % N - N // 2) / N
    phase = np.exp(-1j * np.pi * FRESNEL_DEPTH * frequency**2)
    move = np.conj(transform) @ (phase[:, None] * transform)
    tables = []
    for matrix in (move, transform):
        right = np.block([[matrix.real, matrix.imag], [-matrix.imag, matrix.real]])
        for form in (right, right.T):
            form = form.astype(np.float32)
            high = form.astype(BF16)
            low = (form - high.astype(np.float32)).astype(BF16)
            tables += [high, low]
    return tables


def split(value):
    high = value.astype(BF16)
    return high, (value - high.astype(F32)).astype(BF16)


def dot(a, b):
    return jnp.dot(a, b, preferred_element_type=F32)


def right_mul(value, table):
    high, low = split(value)
    return dot(high, table[0]) + dot(low, table[0]) + dot(high, table[1])


def left_mul(value, table):
    high, low = split(value)
    return dot(table[0], high) + dot(table[0], low) + dot(table[1], high)


def blocks(value):
    return [[value[:N, :N], value[:N, N:]], [value[N:, :N], value[N:, N:]]]


def join(parts):
    return jnp.concatenate([jnp.concatenate(row, axis=1) for row in parts], axis=0)


def list_live(corner_ref, meta):
    slots = corner_ref.shape[0]

    def visit(which):
        def look(source, count):
            slot = source * CAP + which
            row = corner_ref[slot, 0]
            live = (row >= 0).astype(I32)

            @pl.when(live == 1)
            def _():
                meta[0, count] = slot
                meta[1, count] = row
                meta[2, count] = corner_ref[slot, 1]
                meta[3, count] = which
                meta[4, count] = 1

            return count + live

        return look

    n_mate = lax.fori_loop(0, slots // CAP, visit(1), jnp.int32(0))
    count = lax.fori_loop(0, slots // CAP, visit(0), n_mate)
    for extra in range(UNROLL):
        for field in range(5):
            meta[field, count + extra] = 0
    return n_mate, count


def prepare_kernel(me_ref, owners_ref, offsets_ref, amplitudes_ref, out_ref, seen):
    for owner in range(out_ref.shape[0] // CAP):
        seen[owner] = 0
    out_ref[:, N:, :] = jnp.full((out_ref.shape[0], TAIL, N), -1, jnp.int16)
    lane = lax.broadcasted_iota(I32, (TAIL, N), 1)

    def place(position, carry):
        owner = owners_ref[position]
        rank = seen[owner]
        seen[owner] = rank + 1
        core = (owner ^ me_ref[0] ^ rank) & 1
        slot = ((owner & ~1) | core) * CAP + ((owner & 1) ^ core)
        code = jnp.round((amplitudes_ref[position] - AMP_MID) * (1.0 / AMP_STEP))
        out_ref[slot, :N, :] = code.astype(I32).astype(jnp.int16)
        line = jnp.where(lane == 0, offsets_ref[0, position], -1)
        line = jnp.where(lane == 1, offsets_ref[1, position], line)
        out_ref[slot, N:, :] = line.astype(jnp.int16)
        return carry

    lax.fori_loop(0, amplitudes_ref.shape[0], place, 0)


def round_kernel(own_re, own_im, mate_re, mate_im, out_ref):
    for tile, sources in enumerate(((own_re, own_im), (mate_re, mate_im))):

        @pl.when(pl.program_id(0) == tile)
        def _(sources=sources):
            for part, source in enumerate(sources):
                out_ref[0, 0, part] = source[...].astype(BF16).astype(F32)


def positions_kernel(
    corner_ref, codes_ref, tiles_ref, probe_in, tables_ref,
    grad_out, probe_out,
    meta, window, code, patch, high, low, field, inner, back, grad, tables, probe_ref, probe_total,
    window_sem, code_sem, out_sem, table_sem, probe_sem,
):
    table_copy = pltpu.make_async_copy(tables_ref, tables, table_sem)
    table_copy.start()
    probe_copy = pltpu.make_async_copy(probe_in, probe_ref, probe_sem.at[0])
    probe_copy.start()
    _, count = list_live(corner_ref, meta)
    n_groups = (count + UNROLL - 1) // UNROLL

    def window_copies(group, half, start):
        for u in range(UNROLL):
            item = group * UNROLL + u
            row = pl.multiple_of(jnp.minimum(meta[1, item] // 8 * 8, TILE - WIN_ROWS), 8)
            col = jnp.minimum(meta[2, item] // N, 2)
            copy = pltpu.make_async_copy(
                tiles_ref.at[meta[3, item], pl.ds(col, 2), :, :, pl.ds(row, WIN_ROWS)],
                window.at[half, u],
                window_sem.at[half, u],
            )
            copy.start() if start else copy.wait()
            copy = pltpu.make_async_copy(
                codes_ref.at[meta[0, item], pl.ds(0, N)], code.at[half, u], code_sem.at[half, u]
            )
            copy.start() if start else copy.wait()

    def grad_copy(group, half):
        return pltpu.make_async_copy(
            grad.at[half], grad_out.at[pl.ds(group * UNROLL, UNROLL)], out_sem.at[half]
        )

    @pl.when(n_groups > 0)
    def _():
        window_copies(0, 0, True)

    probe_total[...] = jnp.zeros(probe_total.shape, F32)
    lane = lax.broadcasted_iota(I32, (N, N), 1)
    halves = (pl.ds(0, N), pl.ds(N, N))
    table_copy.wait()
    probe_copy.wait()

    def step(group, carry):
        buffer = lax.rem(group, 2)

        @pl.when(group + 1 < n_groups)
        def _():
            window_copies(group + 1, 1 - buffer, True)

        window_copies(group, buffer, False)

        @pl.when(group >= 2)
        def _():
            grad_copy(group - 2, buffer).wait()

        items = [group * UNROLL + u for u in range(UNROLL)]
        where = []
        for item in items:
            row, col = meta[1, item], meta[2, item]
            shift = col - jnp.minimum(col // N, 2) * N
            row_in = row - jnp.minimum(row // 8 * 8, TILE - WIN_ROWS)
            where.append((row_in, shift))

        def put(u, r, c, value):
            big, small = split(value)
            high[u, halves[r], halves[c]] = big
            low[u, halves[r], halves[c]] = small

        def cut(u, layer, part):
            def piece():
                row_in, shift = where[u]
                move = lax.rem(N - shift, N)
                near = window[buffer, u, 0, part, layer, pl.ds(row_in, N), :]
                far = window[buffer, u, 1, part, layer, pl.ds(row_in, N), :]
                both = jnp.where(lane < N - shift, pltpu.roll(near, move, 1), pltpu.roll(far, move, 1))
                patch[u, 2 * layer + part] = both

            return piece

        def swap_blocks(u, source):
            def piece(r, c):
                return lambda: put(u, r, c, source[u, halves[c], halves[r]])

            return [piece(r, c) for r in range(2) for c in range(2)]

        def times_patch(u, layer, load, sign):
            def piece(m, c):
                def work():
                    p_re, p_im = patch[u, 2 * layer], patch[u, 2 * layer + 1]
                    if c == 0:
                        put(u, m, 0, load(m, 0) * p_re - sign * (load(m, 1) * p_im))
                    else:
                        put(u, m, 1, load(m, 1) * p_re + sign * (load(m, 0) * p_im))

                return work

            return [piece(m, c) for m in range(2) for c in range(2)]

        def residual(u):
            def factor():
                power = sum(field[u, halves[c], halves[m]] ** 2 for c in range(2) for m in range(2))
                measured = code[buffer, u].astype(I32).astype(F32) * AMP_STEP + AMP_MID
                live = meta[4, items[u]].astype(F32)
                inner_factor[u] = (1.0 - measured * lax.rsqrt(power + 1.0)) * live

            def piece(c, m):
                return lambda: put(u, c, m, field[u, halves[c], halves[m]] * inner_factor[u])

            return [factor] + [piece(c, m) for c in range(2) for m in range(2)]

        inner_factor = {}

        def add_patch(u, plane, value):
            grad[buffer, u, plane] = value.astype(BF16)

        def exit_gradient(u):
            def wave(c, m):
                return inner[u, halves[c], halves[m]]

            def wake(c, m):
                return back[u, halves[m], halves[c]]

            return [
                lambda: add_patch(
                    u, 2, sum(wave(0, m) * wake(0, m) + wave(1, m) * wake(1, m) for m in range(2))
                ),
                lambda: add_patch(
                    u, 3, sum(wave(0, m) * wake(1, m) - wave(1, m) * wake(0, m) for m in range(2))
                ),
            ]

        def entry_gradient(u):
            def wake(c, m):
                return field[u, halves[c], halves[m]]

            def probe_term(m):
                def work():
                    p_re, p_im = patch[u, 0], patch[u, 1]
                    probe_total[m, 0] += p_re * wake(0, m) + p_im * wake(1, m)
                    probe_total[m, 1] += p_re * wake(1, m) - p_im * wake(0, m)

                return work

            return [
                probe_term(0),
                probe_term(1),
                lambda: add_patch(
                    u,
                    0,
                    sum(
                        probe_ref[m, 0] * wake(0, m) + probe_ref[m, 1] * wake(1, m) for m in range(2)
                    ),
                ),
                lambda: add_patch(
                    u,
                    1,
                    sum(
                        probe_ref[m, 0] * wake(1, m) - probe_ref[m, 1] * wake(0, m) for m in range(2)
                    ),
                ),
            ]

        def from_probe(u):
            return lambda m, c: probe_ref[m, c]

        def from_inner(u):
            return lambda m, c: inner[u, halves[c], halves[m]]

        def from_back(u):
            return lambda m, c: back[u, halves[m], halves[c]]

        stages = (
            ("right", 0, field, lambda u: [cut(u, 0, 0), cut(u, 0, 1)] + times_patch(u, 0, from_probe(u), 1), lambda u: []),
            ("left", 1, inner, lambda u: swap_blocks(u, field), lambda u: [cut(u, 1, 0), cut(u, 1, 1)]),
            ("right", 2, field, lambda u: times_patch(u, 1, from_inner(u), 1), lambda u: []),
            ("left", 3, field, lambda u: swap_blocks(u, field), lambda u: []),
            ("left", 2, field, residual, lambda u: []),
            ("right", 3, back, lambda u: swap_blocks(u, field), lambda u: []),
            ("right", 1, field, lambda u: times_patch(u, 1, from_back(u), -1), lambda u: []),
            ("left", 0, field, lambda u: swap_blocks(u, field), exit_gradient),
        )
        jobs = [(s, u) for s in range(len(stages)) for u in range(UNROLL)]
        for piece in stages[0][3](0):
            piece()
        for at, (s, u) in enumerate(jobs):
            side, form, result, _, beside = stages[s]
            pieces = list(beside(u))
            if at + 1 < len(jobs):
                s_next, u_next = jobs[at + 1]
                pieces = list(stages[s_next][3](u_next)) + pieces
            if s == len(stages) - 1 and u > 0:
                pieces += entry_gradient(u - 1)
            cuts = [(len(pieces) * k + 2) // 3 for k in range(4)]
            big, small = high[u], low[u]
            sums = None
            for k, (data, part) in enumerate(((big, 0), (small, 0), (big, 1))):
                table = tables[2 * form + part]
                product = dot(data, table) if side == "right" else dot(table, data)
                sums = product if sums is None else sums + product
                for piece in pieces[cuts[k] : cuts[k + 1]]:
                    piece()
            result[u] = sums
        for piece in entry_gradient(UNROLL - 1):
            piece()

        grad_copy(group, buffer).start()
        return carry

    lax.fori_loop(0, n_groups, step, 0)
    probe_back = pltpu.make_async_copy(probe_total, probe_out, probe_sem.at[1])
    probe_back.start()
    for before in (2, 1):

        @pl.when(n_groups >= before)
        def _(before=before):
            grad_copy(n_groups - before, lax.rem(n_groups - before, 2)).wait()

    probe_back.wait()


def scatter_kernel(corner_ref, grad_in, own_out, mate_out, meta, grad, total, in_sem, out_sem):
    _, count = list_live(corner_ref, meta)
    n_groups = (count + UNROLL - 1) // UNROLL

    def grad_copy(group):
        items = pl.ds(group * UNROLL, UNROLL)
        return pltpu.make_async_copy(grad_in.at[items], grad.at[items], in_sem.at[group])

    def fetch(group, carry):
        grad_copy(group).start()
        return carry

    def total_copies(layer):
        return [
            pltpu.make_async_copy(
                total.at[tile, pl.ds(2 * layer, 2), side],
                out.at[layer, :, :, pl.ds(side * N, N)],
                out_sem.at[tile, layer, side],
            )
            for tile, out in enumerate((own_out, mate_out))
            for side in range(TILE // N)
        ]

    lax.fori_loop(0, n_groups, fetch, 0)
    total[...] = jnp.zeros(total.shape, F32)
    lane = lax.broadcasted_iota(I32, (N, N), 1)

    for layer in (1, 0):

        def step(group, carry, layer=layer):
            if layer == 1:
                grad_copy(group).wait()
            for u in range(UNROLL):
                item = group * UNROLL + u
                row, col, tile = meta[1, item], meta[2, item], meta[3, item]
                first = jnp.minimum(col // N, 2)
                shift = col - first * N
                for plane in (2 * layer, 2 * layer + 1):
                    moved = pltpu.roll(grad[item, plane].astype(F32), lax.rem(shift, N), 1)
                    here = (tile, plane, first, pl.ds(row, N))
                    there = (tile, plane, first + 1, pl.ds(row, N))
                    total[here] = total[here] + jnp.where(lane >= shift, moved, 0.0)
                    total[there] = total[there] + jnp.where(lane < shift, moved, 0.0)
            return carry

        lax.fori_loop(0, n_groups, step, 0)
        for copy in total_copies(layer):
            copy.start()
    for copy in total_copies(1) + total_copies(0):
        copy.wait()


def spec(space):
    return pl.BlockSpec(memory_space=space)


VMEM, SMEM, HBM, ANY = spec(pltpu.VMEM), spec(pltpu.SMEM), spec(pltpu.HBM), spec(pl.ANY)
PARAMS = pltpu.CompilerParams(vmem_limit_bytes=VMEM_LIMIT)
TWO = 2 * N


def run_round(own_re, own_im, mate_re, mate_im):
    strips = TILE // N

    def index_of(tile):
        idle = strips - 1 if tile == 0 else 0
        return lambda t, strip: (0, 0, jnp.where(t == tile, strip, idle))

    block = (2, TILE, N)
    return pl.pallas_call(
        round_kernel,
        grid=(2, strips),
        out_shape=jax.ShapeDtypeStruct((2, strips, 2, 2, TILE, N), F32),
        in_specs=[pl.BlockSpec(block, index_of(tile)) for tile in (0, 0, 1, 1)],
        out_specs=pl.BlockSpec((1, 1, 2, 2, TILE, N), lambda t, strip: (t, strip, 0, 0, 0, 0)),
        compiler_params=PARAMS,
        cost_estimate=pl.CostEstimate(flops=0, bytes_accessed=16 * 2**20, transcendentals=0),
        name="round",
    )(own_re, own_im, mate_re, mate_im)


def run_positions(corners, codes, tiles, probe, tables):
    slots = codes.shape[0]
    wave = pltpu.VMEM((UNROLL, TWO, TWO), F32)
    half = pltpu.VMEM((UNROLL, TWO, TWO), BF16)
    return pl.pallas_call(
        positions_kernel,
        out_shape=(
            jax.ShapeDtypeStruct((slots, 4, N, N), BF16),
            jax.ShapeDtypeStruct((2, 2, N, N), F32),
        ),
        in_specs=[SMEM] + [ANY] * 4,
        out_specs=(ANY, ANY),
        scratch_shapes=[
            pltpu.SMEM((5, slots + UNROLL), I32),
            pltpu.VMEM((2, UNROLL, 2, 2, 2, WIN_ROWS, N), F32),
            pltpu.VMEM((2, UNROLL, N, N), jnp.int16),
            pltpu.VMEM((UNROLL, 4, N, N), F32),
            half,
            half,
            wave,
            wave,
            wave,
            pltpu.VMEM((2, UNROLL, 4, N, N), BF16),
            pltpu.VMEM((8, TWO, TWO), BF16),
            pltpu.VMEM((2, 2, N, N), F32),
            pltpu.VMEM((2, 2, N, N), F32),
            pltpu.SemaphoreType.DMA((2, UNROLL)),
            pltpu.SemaphoreType.DMA((2, UNROLL)),
            pltpu.SemaphoreType.DMA((2,)),
            pltpu.SemaphoreType.DMA,
            pltpu.SemaphoreType.DMA((2,)),
        ],
        compiler_params=PARAMS,
        cost_estimate=pl.CostEstimate(
            flops=slots * 48 * TWO**3, bytes_accessed=24 * 2**20, transcendentals=0
        ),
        name="positions",
    )(corners, codes, tiles, probe, tables)


def run_scatter(corners, grads):
    slots = grads.shape[0]
    grad_shape = jax.ShapeDtypeStruct((2, 2, TILE, TILE), F32)
    return pl.pallas_call(
        scatter_kernel,
        out_shape=(grad_shape, grad_shape),
        in_specs=[SMEM, ANY],
        out_specs=(ANY, ANY),
        scratch_shapes=[
            pltpu.SMEM((5, slots + UNROLL), I32),
            pltpu.VMEM((slots, 4, N, N), BF16),
            pltpu.VMEM((2, 4, TILE // N, TILE, N), F32),
            pltpu.SemaphoreType.DMA((slots // UNROLL,)),
            pltpu.SemaphoreType.DMA((2, 2, TILE // N)),
        ],
        compiler_params=PARAMS,
        cost_estimate=pl.CostEstimate(flops=0, bytes_accessed=20 * 2**20, transcendentals=0),
        name="scatter",
    )(corners, grads)


def tie(*values):
    return lax.optimization_barrier(values)


def finish(corners, grads, probe_part, pos_dev):
    axes = ("region", "scan")
    devices = lax.axis_size("region") * lax.axis_size("scan")
    mates = [(i, i ^ 1) for i in range(devices)]
    parts = probe_part.reshape(devices, -1, N)
    own_grad, mate_grad = run_scatter(corners, grads)
    pieces = lax.all_to_all(parts, axes, 0, 0, tiled=True)
    piece = jnp.sum(pieces, axis=0, keepdims=True) / pos_dev
    piece, own_grad, mate_grad = tie(piece, own_grad, mate_grad)
    other_grad = lax.ppermute(mate_grad, axes, mates)
    whole = lax.all_to_all(jnp.broadcast_to(piece, parts.shape), axes, 0, 0, tiled=True)
    object_grad = own_grad + other_grad
    whole, object_grad = tie(whole, object_grad)
    return object_grad, whole.reshape(probe_part.shape)


def body(object_real, object_imag, probe_modes, amplitudes, offsets, owners):
    groups = lax.axis_size("scan")
    pos_dev = offsets.shape[0]
    slots = groups * CAP
    mates = [(i, i ^ 1) for i in range(groups)]
    tables = jnp.asarray(np.stack(operator_tables()))
    me = lax.axis_index("scan").astype(I32).reshape(1)

    requests = pl.pallas_call(
        prepare_kernel,
        out_shape=jax.ShapeDtypeStruct((slots, N + TAIL, N), jnp.int16),
        in_specs=[SMEM, SMEM, SMEM, VMEM],
        out_specs=VMEM,
        scratch_shapes=[pltpu.SMEM((groups,), I32)],
        compiler_params=PARAMS,
        name="prepare",
    )(me, owners.reshape(pos_dev), offsets.T, amplitudes)
    arrived = lax.all_to_all(
        requests.reshape(groups, CAP, N + TAIL, N), "scan", 0, 0, tiled=True
    ).reshape(slots, N + TAIL, N)
    mate_real = lax.ppermute(object_real, "scan", mates)
    mate_imag = lax.ppermute(object_imag, "scan", mates)
    tiles = run_round(object_real, object_imag, mate_real, mate_imag)
    arrived, tiles = tie(arrived, tiles)
    corners = arrived[:, N, :2].astype(I32)
    grads, probe_part = run_positions(
        corners, arrived, tiles, probe_modes, tables
    )
    return finish(corners, grads, probe_part, pos_dev)


def solution(mesh):
    return jax.shard_map(
        body,
        mesh=mesh,
        in_specs=(
            P(None, "region", "scan"),
            P(None, "region", "scan"),
            P(),
            P(("region", "scan"), None, None),
            P(("region", "scan"), None),
            P(("region", "scan"), None),
        ),
        out_specs=(P(None, None, "region", "scan"), P()),
        check_vma=False,
    )
```

```python
import functools

import jax
import jax.numpy as jnp
import numpy as np
from jax import lax
from jax.experimental import pallas as pl
from jax.experimental.pallas import tpu as pltpu
from jax.sharding import PartitionSpec as P

BF16 = jnp.bfloat16
F32 = jnp.float32
I32 = jnp.int32

CAP = 2
FRESNEL_DEPTH = 20.0
N = 128
TILE = 512
UNROLL = 4
WIN_ROWS = N + 8
TAIL = 16
AMP_MID = 2.25
AMP_STEP = 1.75 / 32767.0
VMEM_LIMIT = 56 * 2**20


def operator_tables():
    index = np.arange(N)
    transform = np.exp(-2j * np.pi * (np.outer(index, index) % N) / N) / np.sqrt(N)
    frequency = ((index + N // 2) % N - N // 2) / N
    phase = np.exp(-1j * np.pi * FRESNEL_DEPTH * frequency**2)
    move = np.conj(transform) @ (phase[:, None] * transform)
    tables = []
    for matrix in (move, transform):
        right = np.block([[matrix.real, matrix.imag], [-matrix.imag, matrix.real]])
        for form in (right, right.T):
            form = form.astype(np.float32)
            high = form.astype(BF16)
            low = (form - high.astype(np.float32)).astype(BF16)
            tables += [high, low]
    return tables


def split(value):
    high = value.astype(BF16)
    return high, (value - high.astype(F32)).astype(BF16)


def dot(a, b):
    return jnp.dot(a, b, preferred_element_type=F32)


def right_mul(value, table):
    high, low = split(value)
    return dot(high, table[0]) + dot(low, table[0]) + dot(high, table[1])


def left_mul(value, table):
    high, low = split(value)
    return dot(table[0], high) + dot(table[0], low) + dot(table[1], high)


def blocks(value):
    return [[value[:N, :N], value[:N, N:]], [value[N:, :N], value[N:, N:]]]


def join(parts):
    return jnp.concatenate([jnp.concatenate(row, axis=1) for row in parts], axis=0)


def list_live(corner_ref, meta):
    slots = corner_ref.shape[0]

    def visit(which):
        def look(source, count):
            slot = source * CAP + which
            row = corner_ref[slot, 0]
            live = (row >= 0).astype(I32)

            @pl.when(live == 1)
            def _():
                meta[0, count] = slot
                meta[1, count] = row
                meta[2, count] = corner_ref[slot, 1]
                meta[3, count] = which
                meta[4, count] = 1

            return count + live

        return look

    n_mate = lax.fori_loop(0, slots // CAP, visit(1), jnp.int32(0))
    count = lax.fori_loop(0, slots // CAP, visit(0), n_mate)
    for extra in range(UNROLL):
        for field in range(5):
            meta[field, count + extra] = 0
    return n_mate, count


def prepare_kernel(me_ref, owners_ref, offsets_ref, amplitudes_ref, out_ref, seen):
    for owner in range(out_ref.shape[0] // CAP):
        seen[owner] = 0
    out_ref[:, N:, :] = jnp.full((out_ref.shape[0], TAIL, N), -1, jnp.int16)
    lane = lax.broadcasted_iota(I32, (TAIL, N), 1)

    def place(position, carry):
        owner = owners_ref[position]
        rank = seen[owner]
        seen[owner] = rank + 1
        core = (owner ^ me_ref[0] ^ rank) & 1
        slot = ((owner & ~1) | core) * CAP + ((owner & 1) ^ core)
        code = jnp.round((amplitudes_ref[position] - AMP_MID) * (1.0 / AMP_STEP))
        out_ref[slot, :N, :] = code.astype(I32).astype(jnp.int16)
        line = jnp.where(lane == 0, offsets_ref[0, position], -1)
        line = jnp.where(lane == 1, offsets_ref[1, position], line)
        out_ref[slot, N:, :] = line.astype(jnp.int16)
        return carry

    lax.fori_loop(0, amplitudes_ref.shape[0], place, 0)


def round_kernel(own_re, own_im, mate_re, mate_im, out_ref):
    for tile, sources in enumerate(((own_re, own_im), (mate_re, mate_im))):

        @pl.when(pl.program_id(0) == tile)
        def _(sources=sources):
            for part, source in enumerate(sources):
                out_ref[0, 0, part] = source[...].astype(BF16).astype(F32)


def positions_kernel(
    corner_ref, codes_ref, tiles_ref, probe_in, tables_ref,
    grad_out, probe_out,
    meta, window, code, patch, high, low, field, inner, back, grad, tables, probe_ref, probe_total,
    window_sem, code_sem, out_sem, table_sem, probe_sem,
):
    table_copy = pltpu.make_async_copy(tables_ref, tables, table_sem)
    table_copy.start()
    probe_copy = pltpu.make_async_copy(probe_in, probe_ref, probe_sem.at[0])
    probe_copy.start()
    _, count = list_live(corner_ref, meta)
    n_groups = (count + UNROLL - 1) // UNROLL

    def window_copies(group, half, start):
        for u in range(UNROLL):
            item = group * UNROLL + u
            row = pl.multiple_of(jnp.minimum(meta[1, item] // 8 * 8, TILE - WIN_ROWS), 8)
            col = jnp.minimum(meta[2, item] // N, 2)
            copy = pltpu.make_async_copy(
                tiles_ref.at[meta[3, item], pl.ds(col, 2), :, :, pl.ds(row, WIN_ROWS)],
                window.at[half, u],
                window_sem.at[half, u],
            )
            copy.start() if start else copy.wait()
            copy = pltpu.make_async_copy(
                codes_ref.at[meta[0, item], pl.ds(0, N)], code.at[half, u], code_sem.at[half, u]
            )
            copy.start() if start else copy.wait()

    def grad_copy(group, half):
        return pltpu.make_async_copy(
            grad.at[half], grad_out.at[pl.ds(group * UNROLL, UNROLL)], out_sem.at[half]
        )

    @pl.when(n_groups > 0)
    def _():
        window_copies(0, 0, True)

    probe_total[...] = jnp.zeros(probe_total.shape, F32)
    lane = lax.broadcasted_iota(I32, (N, N), 1)
    halves = (pl.ds(0, N), pl.ds(N, N))
    table_copy.wait()
    probe_copy.wait()

    def enter(group, buffer):
        row, col = meta[1, group * UNROLL], meta[2, group * UNROLL]
        shift = col - jnp.minimum(col // N, 2) * N
        row_in = row - jnp.minimum(row // 8 * 8, TILE - WIN_ROWS)

        def cut(part):
            def piece():
                move = lax.rem(N - shift, N)
                near = window[buffer, 0, 0, part, 0, pl.ds(row_in, N), :]
                far = window[buffer, 0, 1, part, 0, pl.ds(row_in, N), :]
                patch[0, part] = jnp.where(
                    lane < N - shift, pltpu.roll(near, move, 1), pltpu.roll(far, move, 1)
                )

            return piece

        def times(m, c):
            def piece():
                p_re, p_im = patch[0, 0], patch[0, 1]
                w_re, w_im = probe_ref[m, 0], probe_ref[m, 1]
                value = w_re * p_re - w_im * p_im if c == 0 else w_im * p_re + w_re * p_im
                big, small = split(value)
                high[0, halves[m], halves[c]] = big
                low[0, halves[m], halves[c]] = small

            return piece

        return [cut(0), cut(1)] + [times(m, c) for m in range(2) for c in range(2)]

    @pl.when(n_groups > 0)
    def _():
        window_copies(0, 0, False)
        for piece in enter(0, 0):
            piece()

    def step(group, carry):
        buffer = lax.rem(group, 2)

        @pl.when(group + 1 < n_groups)
        def _():
            window_copies(group + 1, 1 - buffer, True)

        @pl.when(group >= 2)
        def _():
            grad_copy(group - 2, buffer).wait()

        items = [group * UNROLL + u for u in range(UNROLL)]
        where = []
        for item in items:
            row, col = meta[1, item], meta[2, item]
            shift = col - jnp.minimum(col // N, 2) * N
            row_in = row - jnp.minimum(row // 8 * 8, TILE - WIN_ROWS)
            where.append((row_in, shift))

        def put(u, r, c, value):
            big, small = split(value)
            high[u, halves[r], halves[c]] = big
            low[u, halves[r], halves[c]] = small

        def cut(u, layer, part):
            def piece():
                row_in, shift = where[u]
                move = lax.rem(N - shift, N)
                near = window[buffer, u, 0, part, layer, pl.ds(row_in, N), :]
                far = window[buffer, u, 1, part, layer, pl.ds(row_in, N), :]
                both = jnp.where(lane < N - shift, pltpu.roll(near, move, 1), pltpu.roll(far, move, 1))
                patch[u, 2 * layer + part] = both

            return piece

        def swap_blocks(u, source):
            def piece(r, c):
                return lambda: put(u, r, c, source[u, halves[c], halves[r]])

            return [piece(r, c) for r in range(2) for c in range(2)]

        def times_patch(u, layer, load, sign):
            def piece(m, c):
                def work():
                    p_re, p_im = patch[u, 2 * layer], patch[u, 2 * layer + 1]
                    if c == 0:
                        put(u, m, 0, load(m, 0) * p_re - sign * (load(m, 1) * p_im))
                    else:
                        put(u, m, 1, load(m, 1) * p_re + sign * (load(m, 0) * p_im))

                return work

            return [piece(m, c) for m in range(2) for c in range(2)]

        def residual(u):
            def factor():
                power = sum(field[u, halves[c], halves[m]] ** 2 for c in range(2) for m in range(2))
                measured = code[buffer, u].astype(I32).astype(F32) * AMP_STEP + AMP_MID
                live = meta[4, items[u]].astype(F32)
                inner_factor[u] = (1.0 - measured * lax.rsqrt(power + 1.0)) * live

            def piece(c, m):
                return lambda: put(u, c, m, field[u, halves[c], halves[m]] * inner_factor[u])

            return [factor] + [piece(c, m) for c in range(2) for m in range(2)]

        inner_factor = {}

        def add_patch(u, plane, value):
            grad[buffer, u, plane] = value.astype(BF16)

        def exit_gradient(u):
            def wave(c, m):
                return inner[u, halves[c], halves[m]]

            def wake(c, m):
                return back[u, halves[m], halves[c]]

            return [
                lambda: add_patch(
                    u, 2, sum(wave(0, m) * wake(0, m) + wave(1, m) * wake(1, m) for m in range(2))
                ),
                lambda: add_patch(
                    u, 3, sum(wave(0, m) * wake(1, m) - wave(1, m) * wake(0, m) for m in range(2))
                ),
            ]

        def entry_gradient(u):
            def wake(c, m):
                return field[u, halves[c], halves[m]]

            def probe_term(m):
                def work():
                    p_re, p_im = patch[u, 0], patch[u, 1]
                    probe_total[m, 0] += p_re * wake(0, m) + p_im * wake(1, m)
                    probe_total[m, 1] += p_re * wake(1, m) - p_im * wake(0, m)

                return work

            return [
                probe_term(0),
                probe_term(1),
                lambda: add_patch(
                    u,
                    0,
                    sum(
                        probe_ref[m, 0] * wake(0, m) + probe_ref[m, 1] * wake(1, m) for m in range(2)
                    ),
                ),
                lambda: add_patch(
                    u,
                    1,
                    sum(
                        probe_ref[m, 0] * wake(1, m) - probe_ref[m, 1] * wake(0, m) for m in range(2)
                    ),
                ),
            ]

        def from_probe(u):
            return lambda m, c: probe_ref[m, c]

        def from_inner(u):
            return lambda m, c: inner[u, halves[c], halves[m]]

        def from_back(u):
            return lambda m, c: back[u, halves[m], halves[c]]

        stages = (
            ("right", 0, field, lambda u: [cut(u, 0, 0), cut(u, 0, 1)] + times_patch(u, 0, from_probe(u), 1), lambda u: []),
            ("left", 1, inner, lambda u: swap_blocks(u, field), lambda u: [cut(u, 1, 0), cut(u, 1, 1)]),
            ("right", 2, field, lambda u: times_patch(u, 1, from_inner(u), 1), lambda u: []),
            ("left", 3, field, lambda u: swap_blocks(u, field), lambda u: []),
            ("left", 2, field, residual, lambda u: []),
            ("right", 3, back, lambda u: swap_blocks(u, field), lambda u: []),
            ("right", 1, field, lambda u: times_patch(u, 1, from_back(u), -1), lambda u: []),
            ("left", 0, field, lambda u: swap_blocks(u, field), exit_gradient),
        )
        jobs = [(s, u) for s in range(len(stages)) for u in range(UNROLL)]
        for at, (s, u) in enumerate(jobs):
            side, form, result, _, beside = stages[s]
            pieces = list(beside(u))
            if at + 1 < len(jobs):
                s_next, u_next = jobs[at + 1]
                pieces = list(stages[s_next][3](u_next)) + pieces
            if s == len(stages) - 1 and u > 0:
                pieces += entry_gradient(u - 1)
            if at + 1 == len(jobs):

                @pl.when(group + 1 < n_groups)
                def _():
                    window_copies(group + 1, 1 - buffer, False)

                pieces += enter(group + 1, 1 - buffer)
            cuts = [(len(pieces) * k + 2) // 3 for k in range(4)]
            big, small = high[u], low[u]
            sums = None
            for k, (data, part) in enumerate(((big, 0), (small, 0), (big, 1))):
                table = tables[2 * form + part]
                product = dot(data, table) if side == "right" else dot(table, data)
                sums = product if sums is None else sums + product
                for piece in pieces[cuts[k] : cuts[k + 1]]:
                    piece()
            result[u] = sums
        for piece in entry_gradient(UNROLL - 1):
            piece()

        grad_copy(group, buffer).start()
        return carry

    lax.fori_loop(0, n_groups, step, 0)
    probe_back = pltpu.make_async_copy(probe_total, probe_out, probe_sem.at[1])
    probe_back.start()
    for before in (2, 1):

        @pl.when(n_groups >= before)
        def _(before=before):
            grad_copy(n_groups - before, lax.rem(n_groups - before, 2)).wait()

    probe_back.wait()


def scatter_kernel(corner_ref, grad_in, own_out, mate_out, meta, grad, total, in_sem, out_sem):
    _, count = list_live(corner_ref, meta)
    n_groups = (count + UNROLL - 1) // UNROLL

    def grad_copy(group):
        items = pl.ds(group * UNROLL, UNROLL)
        return pltpu.make_async_copy(grad_in.at[items], grad.at[items], in_sem.at[group])

    def fetch(group, carry):
        grad_copy(group).start()
        return carry

    def total_copies(layer):
        return [
            pltpu.make_async_copy(
                total.at[tile, pl.ds(2 * layer, 2), side],
                out.at[layer, :, :, pl.ds(side * N, N)],
                out_sem.at[tile, layer, side],
            )
            for tile, out in enumerate((own_out, mate_out))
            for side in range(TILE // N)
        ]

    lax.fori_loop(0, n_groups, fetch, 0)
    total[...] = jnp.zeros(total.shape, F32)
    lane = lax.broadcasted_iota(I32, (N, N), 1)

    for layer in (1, 0):

        def step(group, carry, layer=layer):
            if layer == 1:
                grad_copy(group).wait()
            for u in range(UNROLL):
                item = group * UNROLL + u
                row, col, tile = meta[1, item], meta[2, item], meta[3, item]
                first = jnp.minimum(col // N, 2)
                shift = col - first * N
                for plane in (2 * layer, 2 * layer + 1):
                    moved = pltpu.roll(grad[item, plane].astype(F32), lax.rem(shift, N), 1)
                    here = (tile, plane, first, pl.ds(row, N))
                    there = (tile, plane, first + 1, pl.ds(row, N))
                    total[here] = total[here] + jnp.where(lane >= shift, moved, 0.0)
                    total[there] = total[there] + jnp.where(lane < shift, moved, 0.0)
            return carry

        lax.fori_loop(0, n_groups, step, 0)
        for copy in total_copies(layer):
            copy.start()
    for copy in total_copies(1) + total_copies(0):
        copy.wait()


def spec(space):
    return pl.BlockSpec(memory_space=space)


VMEM, SMEM, HBM, ANY = spec(pltpu.VMEM), spec(pltpu.SMEM), spec(pltpu.HBM), spec(pl.ANY)
PARAMS = pltpu.CompilerParams(vmem_limit_bytes=VMEM_LIMIT)
TWO = 2 * N


def run_round(own_re, own_im, mate_re, mate_im):
    strips = TILE // N

    def index_of(tile):
        idle = strips - 1 if tile == 0 else 0
        return lambda t, strip: (0, 0, jnp.where(t == tile, strip, idle))

    block = (2, TILE, N)
    return pl.pallas_call(
        round_kernel,
        grid=(2, strips),
        out_shape=jax.ShapeDtypeStruct((2, strips, 2, 2, TILE, N), F32),
        in_specs=[pl.BlockSpec(block, index_of(tile)) for tile in (0, 0, 1, 1)],
        out_specs=pl.BlockSpec((1, 1, 2, 2, TILE, N), lambda t, strip: (t, strip, 0, 0, 0, 0)),
        compiler_params=PARAMS,
        cost_estimate=pl.CostEstimate(flops=0, bytes_accessed=16 * 2**20, transcendentals=0),
        name="round",
    )(own_re, own_im, mate_re, mate_im)


def run_positions(corners, codes, tiles, probe, tables):
    slots = codes.shape[0]
    wave = pltpu.VMEM((UNROLL, TWO, TWO), F32)
    half = pltpu.VMEM((UNROLL, TWO, TWO), BF16)
    return pl.pallas_call(
        positions_kernel,
        out_shape=(
            jax.ShapeDtypeStruct((slots, 4, N, N), BF16),
            jax.ShapeDtypeStruct((2, 2, N, N), F32),
        ),
        in_specs=[SMEM] + [ANY] * 4,
        out_specs=(ANY, ANY),
        scratch_shapes=[
            pltpu.SMEM((5, slots + UNROLL), I32),
            pltpu.VMEM((2, UNROLL, 2, 2, 2, WIN_ROWS, N), F32),
            pltpu.VMEM((2, UNROLL, N, N), jnp.int16),
            pltpu.VMEM((UNROLL, 4, N, N), F32),
            half,
            half,
            wave,
            wave,
            wave,
            pltpu.VMEM((2, UNROLL, 4, N, N), BF16),
            pltpu.VMEM((8, TWO, TWO), BF16),
            pltpu.VMEM((2, 2, N, N), F32),
            pltpu.VMEM((2, 2, N, N), F32),
            pltpu.SemaphoreType.DMA((2, UNROLL)),
            pltpu.SemaphoreType.DMA((2, UNROLL)),
            pltpu.SemaphoreType.DMA((2,)),
            pltpu.SemaphoreType.DMA,
            pltpu.SemaphoreType.DMA((2,)),
        ],
        compiler_params=PARAMS,
        cost_estimate=pl.CostEstimate(
            flops=slots * 48 * TWO**3, bytes_accessed=24 * 2**20, transcendentals=0
        ),
        name="positions",
    )(corners, codes, tiles, probe, tables)


def run_scatter(corners, grads):
    slots = grads.shape[0]
    grad_shape = jax.ShapeDtypeStruct((2, 2, TILE, TILE), F32)
    return pl.pallas_call(
        scatter_kernel,
        out_shape=(grad_shape, grad_shape),
        in_specs=[SMEM, ANY],
        out_specs=(ANY, ANY),
        scratch_shapes=[
            pltpu.SMEM((5, slots + UNROLL), I32),
            pltpu.VMEM((slots, 4, N, N), BF16),
            pltpu.VMEM((2, 4, TILE // N, TILE, N), F32),
            pltpu.SemaphoreType.DMA((slots // UNROLL,)),
            pltpu.SemaphoreType.DMA((2, 2, TILE // N)),
        ],
        compiler_params=PARAMS,
        cost_estimate=pl.CostEstimate(flops=0, bytes_accessed=20 * 2**20, transcendentals=0),
        name="scatter",
    )(corners, grads)


def tie(*values):
    return lax.optimization_barrier(values)


def finish(corners, grads, probe_part, pos_dev):
    axes = ("region", "scan")
    devices = lax.axis_size("region") * lax.axis_size("scan")
    mates = [(i, i ^ 1) for i in range(devices)]
    parts = probe_part.reshape(devices, -1, N)
    own_grad, mate_grad = run_scatter(corners, grads)
    pieces = lax.all_to_all(parts, axes, 0, 0, tiled=True)
    piece = jnp.sum(pieces, axis=0, keepdims=True) / pos_dev
    piece, own_grad, mate_grad = tie(piece, own_grad, mate_grad)
    other_grad = lax.ppermute(mate_grad, axes, mates)
    whole = lax.all_to_all(jnp.broadcast_to(piece, parts.shape), axes, 0, 0, tiled=True)
    object_grad = own_grad + other_grad
    whole, object_grad = tie(whole, object_grad)
    return object_grad, whole.reshape(probe_part.shape)


def body(object_real, object_imag, probe_modes, amplitudes, offsets, owners):
    groups = lax.axis_size("scan")
    pos_dev = offsets.shape[0]
    slots = groups * CAP
    mates = [(i, i ^ 1) for i in range(groups)]
    tables = jnp.asarray(np.stack(operator_tables()))
    me = lax.axis_index("scan").astype(I32).reshape(1)

    requests = pl.pallas_call(
        prepare_kernel,
        out_shape=jax.ShapeDtypeStruct((slots, N + TAIL, N), jnp.int16),
        in_specs=[SMEM, SMEM, SMEM, VMEM],
        out_specs=VMEM,
        scratch_shapes=[pltpu.SMEM((groups,), I32)],
        compiler_params=PARAMS,
        name="prepare",
    )(me, owners.reshape(pos_dev), offsets.T, amplitudes)
    arrived = lax.all_to_all(
        requests.reshape(groups, CAP, N + TAIL, N), "scan", 0, 0, tiled=True
    ).reshape(slots, N + TAIL, N)
    mate_real = lax.ppermute(object_real, "scan", mates)
    mate_imag = lax.ppermute(object_imag, "scan", mates)
    tiles = run_round(object_real, object_imag, mate_real, mate_imag)
    arrived, tiles = tie(arrived, tiles)
    corners = arrived[:, N, :2].astype(I32)
    grads, probe_part = run_positions(
        corners, arrived, tiles, probe_modes, tables
    )
    return finish(corners, grads, probe_part, pos_dev)


def solution(mesh):
    return jax.shard_map(
        body,
        mesh=mesh,
        in_specs=(
            P(None, "region", "scan"),
            P(None, "region", "scan"),
            P(),
            P(("region", "scan"), None, None),
            P(("region", "scan"), None),
            P(("region", "scan"), None),
        ),
        out_specs=(P(None, None, "region", "scan"), P()),
        check_vma=False,
    )
```
